32 devices in a mesh: dp: 8 (over y, x, core), tensor: 4 (over z).
Axes of the slice: x: 2, y: 2, z: 4, core: 2. Of those that a mesh axis runs over, the one named last changes fastest.
Arguments:
- queries: bfloat16 [4096, 2048], P('dp', 'tensor'), may hold values from -5 to 5
- keys: bfloat16 [4096, 256], P('dp', 'tensor'), may hold values from -5 to 5
- values: bfloat16 [4096, 256], P('dp', 'tensor'), may hold values from -6 to 6
- grad_out: bfloat16 [4096, 4096], P(('dp', 'tensor')), may hold values from -6 to 6
- out_weight: bfloat16 [4096, 2048], P('dp', 'tensor'), may hold values from -0.375 to 0.375
Outputs:
- grad_queries: bfloat16 [4096, 2048], P('dp', 'tensor')
- grad_keys: bfloat16 [4096, 256], P('dp', 'tensor')
- grad_values: bfloat16 [4096, 256], P('dp', 'tensor')
- grad_weight: bfloat16 [4096, 2048], P('dp', 'tensor')
The draws below stay inside these ranges and needn't reach their ends.
All inputs are finite; a program needn't handle non-finite values.
Results may differ from the reference program's by a relative error of at most 0.03.
Values may be sent and summed in bfloat16 or wider, within the bound.
No kernel may reach another device: no remote copies, remote signals or barrier semaphores. Data moves between devices by JAX's collectives and lax.ppermute only.
A program may use at most 64 MiB of HBM per device.

```python
import jax
import jax.numpy as jnp
from jax import lax

HEAD_DIM = 128
HEADS_DEV = 4
WIDTH = 4096
SEQ = 512
HEADS = 16
KV_HEADS = 2
TOKENS = 4096
N_DP = 8


def draw_queries(key, part):
    key = jax.random.fold_in(key, 11)
    shape = (TOKENS, HEADS * HEAD_DIM)
    base = jax.random.truncated_normal(key, -4.5, 4.5, shape, jnp.float32)
    return base.astype(jnp.bfloat16)


def draw_keys(key, part):
    key = jax.random.fold_in(key, 23)
    shape = (TOKENS, KV_HEADS * HEAD_DIM)
    base = jax.random.truncated_normal(key, -4.5, 4.5, shape, jnp.float32)
    return base.astype(jnp.bfloat16)


def strengthened(array, own_key, source, target, blocks, factor):
    def block_of(axis_at):
        return (jnp.arange(array.shape[axis_at]) // (array.shape[axis_at] // blocks)).reshape((-1,) + (1,) * (array.ndim - 1 - axis_at))

    first = jax.random.permutation(own_key, blocks)[block_of(target)]
    second = (block_of(target) + blocks // 2) % blocks
    return jnp.where((block_of(source) == first) | (block_of(source) == second), factor * array, array)


def levels(own_key, extent, split, low, top_value):
    def one(axis_at, shards_of):
        heights = jax.random.uniform(jax.random.fold_in(jax.random.fold_in(own_key, 6), axis_at), (shards_of,), jnp.float32, low / len(split), top_value / len(split))
        return jnp.repeat(jnp.exp(heights), extent[axis_at] // shards_of).reshape((-1,) + (1,) * (len(extent) - axis_at - 1))

    factor_of = one(*split[0])
    for cut in split[1:]:
        factor_of = factor_of * one(*cut)
    return factor_of


def noise(key, extent, deviation, bound, split=(), kind=jnp.bfloat16):
    values = deviation * jax.random.normal(key, extent, jnp.float32)
    if split:
        values = values * levels(key, extent, split, -0.22, 0.18)
    return jnp.clip(values, -bound, bound).astype(kind)


def noise_with(own_key, dims, scale, most, split, heavy, kind=jnp.bfloat16):
    array = scale * jax.random.normal(own_key, dims, jnp.float32)
    if split:
        array = array * levels(own_key, dims, split, -0.22, 0.18)
    return jnp.clip(strengthened(array, jax.random.fold_in(own_key, 3), *heavy), -most, most).astype(kind)


def setup_inputs(seed: int = 0) -> dict:
    arg_keys = jax.random.split(jax.random.key(seed), 6)
    return {
        "queries": draw_queries(jax.random.fold_in(arg_keys[5], 71), 0),
        "keys": draw_keys(jax.random.fold_in(arg_keys[5], 71), 0),
        "values": noise(arg_keys[2], (TOKENS, KV_HEADS * HEAD_DIM), 1.0, 6.0, ((0, 8), (1, 4))),
        "grad_out": noise_with(arg_keys[3], (TOKENS, WIDTH), 0.25, 6.0, ((0, 32),), (0, 1, 32, 2.75)),
        "out_weight": noise(arg_keys[4], (WIDTH, HEADS * HEAD_DIM), (WIDTH // 16) ** -0.5, 0.375, ((0, 8), (1, 4))),
    }


def rounded(value):
    return lax.optimization_barrier(value.astype(jnp.bfloat16)).astype(jnp.float32)


def reference(queries, keys, values, grad_out, out_weight):
    scale = HEAD_DIM ** -0.5
    query_seqs = queries.reshape(N_DP, SEQ, HEADS * HEAD_DIM)
    key_seqs = keys.reshape(N_DP, SEQ, KV_HEADS * HEAD_DIM)
    value_seqs = values.reshape(N_DP, SEQ, KV_HEADS * HEAD_DIM)
    grad_seqs = grad_out.reshape(N_DP, SEQ, WIDTH)
    positions = jnp.arange(SEQ, dtype=jnp.int32)
    causal = positions[None, :] <= positions[:, None]

    def sequence_grads(carry, inputs):
        query, key_rows, value_rows, grad_rows = inputs
        query_f = query.astype(jnp.float32).reshape(SEQ, KV_HEADS, 2, HEADS_DEV, HEAD_DIM)
        key_f = key_rows.astype(jnp.float32).reshape(SEQ, KV_HEADS, HEAD_DIM)
        value_f = value_rows.astype(jnp.float32).reshape(SEQ, KV_HEADS, HEAD_DIM)
        scores = jnp.einsum("sgpmd,tgd->gpmst", query_f, key_f) * scale
        scores = jnp.where(causal, scores, -jnp.inf)
        probs = jax.nn.softmax(scores, axis=-1)
        probs_half = probs.astype(jnp.bfloat16).astype(jnp.float32)
        attended = jnp.einsum("gpmst,tgd->sgpmd", probs_half, value_f).astype(jnp.bfloat16)
        attended = attended.reshape(SEQ, HEADS * HEAD_DIM)
        grad_att = jnp.dot(grad_rows, out_weight, preferred_element_type=jnp.float32).astype(jnp.bfloat16)
        grad_att_f = grad_att.astype(jnp.float32).reshape(SEQ, KV_HEADS, 2, HEADS_DEV, HEAD_DIM)
        dprobs = jnp.einsum("sgpmd,tgd->gpmst", grad_att_f, value_f)
        delta = jnp.sum(probs * dprobs, axis=-1, keepdims=True)
        dscores = (probs * (dprobs - delta) * scale).astype(jnp.bfloat16).astype(jnp.float32)
        grad_q = jnp.einsum("gpmst,tgd->sgpmd", dscores, key_f).astype(jnp.bfloat16)
        key_part = rounded(jnp.einsum("gpmst,sgpmd->tgpd", dscores, query_f))
        value_part = rounded(jnp.einsum("gpmst,sgpmd->tgpd", probs_half, grad_att_f))
        grad_k = jnp.sum(key_part, axis=2).astype(jnp.bfloat16).reshape(SEQ, KV_HEADS * HEAD_DIM)
        grad_v = jnp.sum(value_part, axis=2).astype(jnp.bfloat16).reshape(SEQ, KV_HEADS * HEAD_DIM)
        term = lax.dot_general(grad_rows, attended, (((0,), (0,)), ((), ())), preferred_element_type=jnp.float32)
        carry = carry + rounded(term)
        return carry, (grad_q.reshape(SEQ, HEADS * HEAD_DIM), grad_k, grad_v)

    start = jnp.zeros((WIDTH, HEADS * HEAD_DIM), jnp.float32)
    total, (grad_q, grad_k, grad_v) = lax.scan(sequence_grads, start, (query_seqs, key_seqs, value_seqs, grad_seqs))
    grad_queries = grad_q.reshape(TOKENS, HEADS * HEAD_DIM)
    grad_keys = grad_k.reshape(TOKENS, KV_HEADS * HEAD_DIM)
    grad_values = grad_v.reshape(TOKENS, KV_HEADS * HEAD_DIM)
    return grad_queries, grad_keys, grad_values, total.astype(jnp.bfloat16)
```

```python
import functools
import math

import jax
import jax.numpy as jnp
from jax import lax
from jax.experimental import pallas as pl
from jax.experimental.pallas import tpu as pltpu
from jax.sharding import PartitionSpec as P

HEAD_DIM = 128
BLOCK = 128
VMEM_BYTES = 20 * 1024 * 1024
SLOTS = 4
SCALE = HEAD_DIM ** (-0.5)
SCALE2 = SCALE * math.log2(math.e)
VMEM = pl.BlockSpec(memory_space=pltpu.VMEM)
SMEM = pl.BlockSpec(memory_space=pltpu.SMEM)
F32 = jnp.float32
BF16 = jnp.bfloat16


def call(kernel, outs, args, flops, scratch=(), scalars=0):
    size = sum(math.prod(a.shape) * a.dtype.itemsize for a in list(args) + list(outs))
    return pl.pallas_call(
        kernel,
        out_shape=tuple(outs),
        in_specs=[SMEM] * scalars + [VMEM] * (len(args) - scalars),
        out_specs=tuple([VMEM] * len(outs)),
        scratch_shapes=list(scratch),
        cost_estimate=pl.CostEstimate(flops=flops, bytes_accessed=size // 100, transcendentals=0),
        compiler_params=pltpu.CompilerParams(vmem_limit_bytes=VMEM_BYTES),
    )(*args)


def dot(a, b, ca, cb):
    return lax.dot_general(a, b, (((ca,), (cb,)), ((), ())), preferred_element_type=F32)


def prep_kernel(order, place, keys, values, grad, own, own_kv, give):
    core, chip = place[0], place[1]
    chips, rows, width = own.shape
    half, length = keys.shape
    for k, s in enumerate(order):
        first = (chip ^ s) * 2
        own[k] = grad[:, pl.ds(pl.multiple_of((first + core) * width, 128), width)]
        own_kv[k * rows : (k + 1) * rows, :] = own[k]
        give[k] = grad[:, pl.ds(pl.multiple_of((first + 1 - core) * width, 128), width)]
    for i in range(length // width):
        at = chips * rows + i * 2 * half
        own_kv[at : at + half, :] = keys[:, i * width : (i + 1) * width]
        own_kv[at + half : at + 2 * half, :] = values[:, i * width : (i + 1) * width]


def forward_kernel(place, queries, keys, values, near, kv, attended, lse):
    parity = place[2]
    half, length = keys.shape
    depth = near.shape[1]
    mine = pl.multiple_of(parity * half, half)
    theirs = pl.multiple_of((1 - parity) * half, half)
    tail = near.shape[0] - length // depth * 2 * half
    for part, ref in enumerate((keys, values)):
        kv[part, pl.ds(mine, half), :] = ref[...]
        for i in range(length // depth):
            at = tail + (2 * i + part) * half
            kv[part, pl.ds(theirs, half), i * depth : (i + 1) * depth] = near[at : at + half, :]
    length, width = queries.shape
    row = lax.broadcasted_iota(jnp.int32, (BLOCK, BLOCK), 0)
    col = lax.broadcasted_iota(jnp.int32, (BLOCK, BLOCK), 1)
    for i in range(length // BLOCK):
        rows = pl.ds(i * BLOCK, BLOCK)
        keys = (i + 1) * BLOCK
        stats = []
        for h in range(width // HEAD_DIM):
            cols = pl.ds(h * HEAD_DIM, HEAD_DIM)
            scores = dot(queries[rows, cols], kv[0, :, :keys], 1, 0) * SCALE2
            last = jnp.where(col <= row, scores[:, keys - BLOCK :], -jnp.inf)
            top = jnp.max(last, axis=1, keepdims=True)
            if i:
                top = jnp.maximum(top, jnp.max(scores[:, : keys - BLOCK], axis=1, keepdims=True))
            powers = jnp.exp2(last - top)
            total = jnp.sum(powers, axis=1, keepdims=True)
            if i:
                early = jnp.exp2(scores[:, : keys - BLOCK] - top)
                total = total + jnp.sum(early, axis=1, keepdims=True)
                powers = jnp.concatenate([early, powers], axis=1)
            probs = (powers / total).astype(BF16)
            attended[rows, cols] = dot(probs, kv[1, :, :keys], 1, 1).astype(BF16)
            stats.append(jnp.broadcast_to(top + jnp.log2(total), (BLOCK, HEAD_DIM)))
        lane = lax.broadcasted_iota(jnp.int32, (BLOCK, HEAD_DIM), 1)
        packed = stats[0]
        for h, stat in enumerate(stats):
            packed = jnp.where(lane == h, stat, packed)
        lse[rows, :] = packed


def backward_kernel(first, final, base, place, queries, kv, lse, grad_own, grad_other, *refs):
    if not first:
        early_q, early_k, early_v = refs[:3]
        refs = refs[3:]
    if final:
        grad_q, keep, send, dk, dv, ds_all, p_all = refs
    else:
        grad_q, dk, dv, ds_all, p_all = refs
    if first:
        dk[...] = jnp.zeros_like(dk)
        dv[...] = jnp.zeros_like(dv)
    else:
        grad_q[...] = early_q[...]
        dk[...] = early_k[...]
        dv[...] = early_v[...]
    length, width = queries.shape
    heads = width // HEAD_DIM
    count, size, _ = grad_own.shape
    row = lax.broadcasted_iota(jnp.int32, (size, BLOCK), 0)
    col = lax.broadcasted_iota(jnp.int32, (size, BLOCK), 1)

    def block(slot, j):
        rows = pl.ds(j * size, size)
        keys = -(-(j + 1) * size // BLOCK) * BLOCK
        early = keys - BLOCK
        grads = []
        for h in range(heads):
            cols = pl.ds(h * HEAD_DIM, HEAD_DIM)
            grad = grad_own[slot, :, cols] + grad_other[slot, :, cols].astype(F32)
            grad = grad.astype(BF16)
            grads.append(grad)
            scores = dot(queries[rows, cols], kv[0, :, :keys], 1, 0) * SCALE2
            probs = jnp.exp2(scores - lse[rows, h : h + 1])
            last = jnp.where(col + early <= row + j * size, probs[:, early:], 0.0)
            probs = jnp.concatenate([probs[:, :early], last], axis=1) if early else last
            dprobs = dot(grad, kv[1, :, :keys], 1, 0)
            delta = jnp.sum(probs * dprobs, axis=1, keepdims=True)
            dscores = (probs * (dprobs - delta) * SCALE).astype(BF16)
            grad_q[rows, cols] = dot(dscores, kv[0, :, :keys], 1, 1).astype(BF16)
            ds_all[pl.ds(h * size, size), :keys] = dscores
            p_all[pl.ds(h * size, size), :keys] = probs.astype(BF16)
        stacked_q = jnp.concatenate(
            [queries[rows, h * HEAD_DIM : (h + 1) * HEAD_DIM] for h in range(heads)], axis=0
        )
        stacked_g = jnp.concatenate(grads, axis=0)
        dk[:, :keys] += dot(stacked_q, ds_all[:, :keys], 0, 0)
        dv[:, :keys] += dot(stacked_g, p_all[:, :keys], 0, 0)

    def step(slot, carry):
        for j in range(length // size):
            pl.when(place[SLOTS + base + slot] == j)(functools.partial(block, slot, j))
        return carry

    lax.fori_loop(0, count, step, 0)
    if final:
        half = HEAD_DIM // 2
        mine = pl.ds(pl.multiple_of(place[2] * half, half), half)
        theirs = pl.ds(pl.multiple_of((1 - place[2]) * half, half), half)
        keep[:half] = dk[mine, :]
        keep[half:] = dv[mine, :]
        send[:half] = dk[theirs, :].astype(BF16)
        send[half:] = dv[theirs, :].astype(BF16)


def finish_kernel(keep, other, partial, *refs):
    received, (grad_k, grad_v, grad_weight) = refs[:-3], refs[-3:]
    half = keep.shape[0] // 2
    total = (keep[...].astype(BF16).astype(F32) + other[...].astype(F32)).astype(BF16)
    grad_k[...] = total[:half]
    grad_v[...] = total[half:]
    total = partial[...]
    for ref in received:
        total = total + ref[...].astype(F32)
    grad_weight[...] = total.astype(BF16)


def chunk(ref, c, rows):
    return ref[c] if len(ref.shape) == 3 else ref[c * rows : (c + 1) * rows, :]


def merge_kernel(first, second, *halves):
    rows = second.shape[1]
    c = 0
    for half in halves:
        for i in range(half.shape[0]):
            half[i, :rows] = chunk(first, c, rows)
            half[i, rows:] = second[c]
            c += 1


def pieces(place, refs, c):
    rows = refs[1].shape[1]
    both = [
        jnp.concatenate([chunk(refs[i], c, rows), refs[i + 1][c]], axis=0)
        for i in range(0, len(refs), 2)
    ]
    if len(both) != 4:
        return both
    inner = (place[3] == 1) | (place[3] == 2)
    return both[:2] + [jnp.where(inner, both[2], both[3])]


def late_piece(place, refs, i):
    inner = (place[3] == 1) | (place[3] == 2)
    return jnp.where(inner, refs[0][i], refs[1][i])


def attended_rows(att_own, att_other, j, rows):
    at = pl.ds(pl.multiple_of(j * rows, rows), rows)
    return jnp.concatenate([att_own[at, :], att_other[at, :]], axis=0)


def early_kernel(count, place, *refs):
    blocks, weights, (own, give) = refs[:count], refs[count:-2], refs[-2:]
    rows = own.shape[1]
    totals = None
    for c, weight in enumerate(weights):
        products = [dot(value, weight[...], 1, 0) for value in pieces(place, blocks, c)]
        totals = [a + b for a, b in zip(totals, products)] if totals else products
    for i, total in enumerate(totals):
        own[i] = total[:rows]
        give[i] = total[rows:].astype(BF16)


def early_term_kernel(count, place, att_own, att_other, *refs):
    blocks, outs = refs[:count], refs[count:]
    rows = blocks[1].shape[1]
    for c, out in enumerate(outs):
        total = None
        for i, value in enumerate(pieces(place, blocks, c)):
            product = dot(value, attended_rows(att_own, att_other, place[SLOTS + i], rows), 0, 0)
            total = product if total is None else total + product
        out[...] = total.astype(BF16)


def late_kernel(sizes, steps, first, place, *refs):
    late, refs = refs[: 2 * len(steps)], refs[2 * len(steps) :]
    count = sum(sizes[side] for side in steps)
    weights, refs = refs[:count], refs[count:]
    total = None if first else refs[0][...]
    c = 0
    for n, side in enumerate(steps):
        for i in range(sizes[side]):
            value = late_piece(place, late[2 * n : 2 * n + 2], i)
            product = dot(value, weights[c][...], 1, 0)
            total = product if total is None else total + product
            c += 1
    if first:
        refs[0][...] = total
    else:
        own, give = refs[1:]
        rows = own.shape[1]
        own[0] = total[:rows]
        give[0] = total[rows:].astype(BF16)


def term_kernel(i, late, spans, place, att_own, att_other, partial, *refs):
    received, outs = refs[late : late + len(spans)], refs[late + len(spans) :]
    total = partial[...].astype(F32)
    if late:
        value = late_piece(place, refs[:late], i)
        rhs = attended_rows(att_own, att_other, place[place.shape[0] - 1], value.shape[0] // 2)
        total = total + dot(value, rhs, 0, 0)
    middle = total.shape[0] // 2
    sides = [total[:middle], total[middle:]]
    for ref, span in zip(received, spans):
        for side in span:
            part = ref[...] if len(span) == 1 else ref[side * middle : (side + 1) * middle]
            sides[side] = sides[side] + part.astype(F32)
    if len(outs) == 2:
        for out, side in zip(outs, sides):
            out[...] = side.astype(out.dtype)
    else:
        outs[0][:middle] = sides[0].astype(outs[0].dtype)
        outs[0][middle:] = sides[1].astype(outs[0].dtype)


def tie(value, *others):
    return lax.optimization_barrier((value, *others))[0]


def body(queries, keys, values, grad_out, out_weight):
    dp, tensor = lax.axis_size("dp"), lax.axis_size("tensor")
    chips = dp // 2
    length, width = queries.shape
    half = keys.shape[1]
    rows = grad_out.shape[0]
    depth = out_weight.shape[0]
    index, part = lax.axis_index("dp"), lax.axis_index("tensor")
    if tensor == 4:
        inner = (part == 1) | (part == 2)
        early = 3
        slots = [0, 1, jnp.where(inner, 3, 2), jnp.where(inner, 2, 3)]
    else:
        early = tensor
        slots = list(range(tensor))
    place = jnp.stack(
        [index % 2, index // 2, part % 2, part] + [part ^ k for k in slots]
    ).astype(jnp.int32)

    def swap(value, axis, mask):
        return lax.ppermute(value, axis, [(i, i ^ mask) for i in range(lax.axis_size(axis))])

    def across(value):
        return lax.ppermute(value, "tensor", [(1, 2), (2, 1)])

    def outward(value):
        return lax.ppermute(value, "tensor", [(1, 0), (2, 3)])

    shape = jax.ShapeDtypeStruct
    order = sorted(range(chips), key=lambda s: (-s.bit_count(), s))
    half_block = shape((chips, rows, depth), BF16)
    tail = length // depth * 2 * half
    own, own_kv, give = call(
        functools.partial(prep_kernel, order),
        [half_block, shape((chips * rows + tail, depth), BF16), half_block],
        [place, keys.T, values.T, grad_out],
        0,
        scalars=1,
    )
    taken = swap(give, "dp", 1)

    near = [swap(own_kv, "tensor", 1), swap(taken, "tensor", 1)]
    weights = {0: out_weight}
    for s in reversed(order[:-1]):
        operand = tie(out_weight, near[0]) if s & (s - 1) else out_weight
        weights[s] = swap(operand, "dp", 2 * s)
    weights = [weights[s] for s in order]

    blocks = [own_kv, taken] + near
    late, second = [], []
    sizes = [1, chips - 2, 1] if chips > 2 else [1] * chips
    flops = 4 * length * depth * width // 100
    if tensor == 4:
        middle_own = across(own)
        direct = [w for s, w in zip(order, weights) if s & (s - 1) == 0]
        middle_taken = across(tie(taken, middle_own, near[0]))
        hold = []
        kv, attended, lse = call(
            forward_kernel,
            [
                shape((2, HEAD_DIM, length), BF16),
                shape((length, width), BF16),
                shape((length, HEAD_DIM), F32),
            ],
            [place, tie(queries, *hold), keys.T, values.T, near[0]],
            4 * length * length * width // 100,
            scalars=1,
        )
        in_own = outward(middle_own)
        in_taken = outward(tie(middle_taken, near[1]))
        blocks += [middle_own, middle_taken, in_own, in_taken]
        att_other = swap(attended, "dp", 1)
        relay = call(
            merge_kernel,
            [shape((size, 2 * rows, depth), BF16) for size in sizes],
            near,
            400 * flops,
        )
        after = [[middle_taken, attended, *direct], [in_own, weights[0], att_other], []]
        for side in range(len(sizes)):
            second.append(across(tie(relay[side], *after[side], *second[-1:])))
    else:
        hold = []
        kv, attended, lse = call(
            forward_kernel,
            [
                shape((2, HEAD_DIM, length), BF16),
                shape((length, width), BF16),
                shape((length, HEAD_DIM), F32),
            ],
            [place, tie(queries, *hold), keys.T, values.T, near[0]],
            4 * length * length * width // 100,
            scalars=1,
        )
        att_other = swap(attended, "dp", 1)
        for k in range(2, tensor):
            blocks += [swap(own, "tensor", k), swap(taken, "tensor", k)]
    grad_own, grad_give = call(
        functools.partial(early_kernel, len(blocks)),
        [shape((early, rows, width), F32), shape((early, rows, width), BF16)],
        [place] + blocks + weights,
        300 * flops,
        scalars=1,
    )
    partials = call(
        functools.partial(early_term_kernel, len(blocks)),
        [shape((depth, width), BF16)] * chips,
        [tie(place, grad_give), attended, att_other] + blocks,
        flops,
        scalars=1,
    )
    grad_other = swap(grad_give, "dp", 1)
    if tensor == 4:
        after = [[], [in_taken, partials[0]], []]
        for side, size in enumerate(sizes):
            arrived = outward(tie(second[side], *after[side]))
            late += [(i, [second[side], arrived]) for i in range(size)]
    else:
        late = [(0, [])] * chips

    def backward(first, final, base, own, other, carry):
        state = [shape((HEAD_DIM, length), F32)] * 2
        ends = [shape((2 * half, length), F32), shape((2 * half, length), BF16)]
        size = (width // HEAD_DIM * rows, length)
        scratch = [pltpu.VMEM(size, BF16)] * 2
        if final:
            scratch = [pltpu.VMEM((HEAD_DIM, length), F32)] * 2 + scratch
        return call(
            functools.partial(backward_kernel, first, final, base),
            [shape((length, width), BF16)] + (ends if final else state),
            [place, queries, kv, lse, own, other] + carry,
            flops,
            scratch=scratch,
            scalars=1,
        )

    received = {s: [] for s in order}

    def term(c, *others, kind=BF16):
        s = order[c]
        low, high = s & -s, 1 << s.bit_length() >> 1
        spans, extra = zip(*received[s]) if received[s] and s else ((), ())
        shapes = [(depth, width)] if low == high else [(depth // 2, width)] * 2
        found = call(
            functools.partial(term_kernel, late[c][0], len(late[c][1]), spans),
            [shape(size, kind) for size in shapes],
            [tie(place, *others), attended, att_other, partials[c]]
            + late[c][1]
            + list(extra),
            300 * flops,
            scalars=1,
        )
        if len(found) == 2:
            received[s ^ low].append(((0,), swap(found[0], "dp", 2 * low)))
            received[s ^ high].append(((1,), swap(found[1], "dp", 2 * high)))
        elif s:
            received[0].append(((0, 1), swap(found[0], "dp", 2 * s)))
        return found[0]

    terms = [term(0)]
    done = backward(
        True,
        early == tensor,
        0,
        grad_own,
        tie(grad_other, terms[0]),
        [],
    )
    terms += [term(c, done[1]) for c in range(1, chips - 1)]

    if tensor == 4:
        pairs = [pair for i, pair in late if i == 0]
        steps = list(range(len(sizes)))
        (total,) = call(
            functools.partial(late_kernel, sizes, steps[:-1], True),
            [shape((2 * rows, width), F32)],
            [tie(place, terms[-1])] + sum(pairs[:-1], []) + weights[: -sizes[-1]],
            flops,
            scalars=1,
        )
        grad_own, grad_give = call(
            functools.partial(late_kernel, sizes, steps[-1:], False),
            [shape((1, rows, width), F32), shape((1, rows, width), BF16)],
            [place] + pairs[-1] + weights[-sizes[-1] :] + [total],
            flops,
            scalars=1,
        )
        grad_other = swap(grad_give, "dp", 1)
        done = backward(False, True, early, grad_own, grad_other, list(done))
    grad_q, keep, send = done
    grad_k, grad_v, grad_weight = call(
        finish_kernel,
        [shape((half, length), BF16)] * 2 + [shape((depth, width), BF16)],
        [keep, swap(send, "tensor", 1), term(chips - 1, kind=F32)]
        + [value for _, value in received[0]],
        flops,
    )
    return grad_q, grad_k.T, grad_v.T, grad_weight


def solution(mesh):
    placed = (
        P("dp", "tensor"),
        P("dp", "tensor"),
        P("dp", "tensor"),
        P(("dp", "tensor"), None),
        P("dp", "tensor"),
    )
    return jax.shard_map(
        body,
        mesh=mesh,
        in_specs=placed,
        out_specs=(P("dp", "tensor"), P("dp", "tensor"), P("dp", "tensor"), P("dp", "tensor")),
        check_vma=False,
    )
```

```python
import functools
import math

import jax
import jax.numpy as jnp
from jax import lax
from jax.experimental import pallas as pl
from jax.experimental.pallas import tpu as pltpu
from jax.sharding import PartitionSpec as P

HEAD_DIM = 128
BLOCK = 128
VMEM_BYTES = 20 * 1024 * 1024
SLOTS = 4
SCALE = HEAD_DIM ** (-0.5)
SCALE2 = SCALE * math.log2(math.e)
VMEM = pl.BlockSpec(memory_space=pltpu.VMEM)
SMEM = pl.BlockSpec(memory_space=pltpu.SMEM)
F32 = jnp.float32
BF16 = jnp.bfloat16


def call(kernel, outs, args, flops, scratch=(), scalars=0):
    size = sum(math.prod(a.shape) * a.dtype.itemsize for a in list(args) + list(outs))
    return pl.pallas_call(
        kernel,
        out_shape=tuple(outs),
        in_specs=[SMEM] * scalars + [VMEM] * (len(args) - scalars),
        out_specs=tuple([VMEM] * len(outs)),
        scratch_shapes=list(scratch),
        cost_estimate=pl.CostEstimate(flops=flops, bytes_accessed=size // 100, transcendentals=0),
        compiler_params=pltpu.CompilerParams(vmem_limit_bytes=VMEM_BYTES),
    )(*args)


def dot(a, b, ca, cb):
    return lax.dot_general(a, b, (((ca,), (cb,)), ((), ())), preferred_element_type=F32)


def prep_kernel(order, place, keys, values, grad, own, own_kv, give):
    core, chip = place[0], place[1]
    chips, rows, width = own.shape
    half, length = keys.shape
    for k, s in enumerate(order):
        first = (chip ^ s) * 2
        own[k] = grad[:, pl.ds(pl.multiple_of((first + core) * width, 128), width)]
        own_kv[k * rows : (k + 1) * rows, :] = own[k]
        give[k] = grad[:, pl.ds(pl.multiple_of((first + 1 - core) * width, 128), width)]
    for i in range(length // width):
        at = chips * rows + i * 2 * half
        own_kv[at : at + half, :] = keys[:, i * width : (i + 1) * width]
        own_kv[at + half : at + 2 * half, :] = values[:, i * width : (i + 1) * width]


def forward_kernel(place, queries, keys, values, near, kv, attended, lse):
    parity = place[2]
    half, length = keys.shape
    depth = near.shape[1]
    mine = pl.multiple_of(parity * half, half)
    theirs = pl.multiple_of((1 - parity) * half, half)
    tail = near.shape[0] - length // depth * 2 * half
    for part, ref in enumerate((keys, values)):
        kv[part, pl.ds(mine, half), :] = ref[...]
        for i in range(length // depth):
            at = tail + (2 * i + part) * half
            kv[part, pl.ds(theirs, half), i * depth : (i + 1) * depth] = near[at : at + half, :]
    length, width = queries.shape
    row = lax.broadcasted_iota(jnp.int32, (BLOCK, BLOCK), 0)
    col = lax.broadcasted_iota(jnp.int32, (BLOCK, BLOCK), 1)
    for i in range(length // BLOCK):
        rows = pl.ds(i * BLOCK, BLOCK)
        keys = (i + 1) * BLOCK
        stats = []
        for h in range(width // HEAD_DIM):
            cols = pl.ds(h * HEAD_DIM, HEAD_DIM)
            scores = dot(queries[rows, cols], kv[0, :, :keys], 1, 0) * SCALE2
            last = jnp.where(col <= row, scores[:, keys - BLOCK :], -jnp.inf)
            top = jnp.max(last, axis=1, keepdims=True)
            if i:
                top = jnp.maximum(top, jnp.max(scores[:, : keys - BLOCK], axis=1, keepdims=True))
            powers = jnp.exp2(last - top)
            total = jnp.sum(powers, axis=1, keepdims=True)
            if i:
                early = jnp.exp2(scores[:, : keys - BLOCK] - top)
                total = total + jnp.sum(early, axis=1, keepdims=True)
                powers = jnp.concatenate([early, powers], axis=1)
            probs = (powers / total).astype(BF16)
            attended[rows, cols] = dot(probs, kv[1, :, :keys], 1, 1).astype(BF16)
            stats.append(jnp.broadcast_to(top + jnp.log2(total), (BLOCK, HEAD_DIM)))
        lane = lax.broadcasted_iota(jnp.int32, (BLOCK, HEAD_DIM), 1)
        packed = stats[0]
        for h, stat in enumerate(stats):
            packed = jnp.where(lane == h, stat, packed)
        lse[rows, :] = packed


def backward_kernel(first, final, base, place, queries, kv, lse, grad_own, grad_other, *refs):
    if not first:
        early_q, early_k, early_v = refs[:3]
        refs = refs[3:]
    if final:
        grad_q, keep, send, dk, dv, ds_all, p_all = refs
    else:
        grad_q, dk, dv, ds_all, p_all = refs
    if first:
        dk[...] = jnp.zeros_like(dk)
        dv[...] = jnp.zeros_like(dv)
    else:
        grad_q[...] = early_q[...]
        dk[...] = early_k[...]
        dv[...] = early_v[...]
    length, width = queries.shape
    heads = width // HEAD_DIM
    count, size, _ = grad_own.shape
    row = lax.broadcasted_iota(jnp.int32, (size, BLOCK), 0)
    col = lax.broadcasted_iota(jnp.int32, (size, BLOCK), 1)

    def block(slot, j):
        rows = pl.ds(j * size, size)
        keys = -(-(j + 1) * size // BLOCK) * BLOCK
        early = keys - BLOCK
        grads = []
        for h in range(heads):
            cols = pl.ds(h * HEAD_DIM, HEAD_DIM)
            grad = grad_own[slot, :, cols] + grad_other[slot, :, cols].astype(F32)
            grad = grad.astype(BF16)
            grads.append(grad)
            scores = dot(queries[rows, cols], kv[0, :, :keys], 1, 0) * SCALE2
            probs = jnp.exp2(scores - lse[rows, h : h + 1])
            last = jnp.where(col + early <= row + j * size, probs[:, early:], 0.0)
            probs = jnp.concatenate([probs[:, :early], last], axis=1) if early else last
            dprobs = dot(grad, kv[1, :, :keys], 1, 0)
            delta = jnp.sum(probs * dprobs, axis=1, keepdims=True)
            dscores = (probs * (dprobs - delta) * SCALE).astype(BF16)
            grad_q[rows, cols] = dot(dscores, kv[0, :, :keys], 1, 1).astype(BF16)
            ds_all[pl.ds(h * size, size), :keys] = dscores
            p_all[pl.ds(h * size, size), :keys] = probs.astype(BF16)
        stacked_q = jnp.concatenate(
            [queries[rows, h * HEAD_DIM : (h + 1) * HEAD_DIM] for h in range(heads)], axis=0
        )
        stacked_g = jnp.concatenate(grads, axis=0)
        dk[:, :keys] += dot(stacked_q, ds_all[:, :keys], 0, 0)
        dv[:, :keys] += dot(stacked_g, p_all[:, :keys], 0, 0)

    def step(slot, carry):
        for j in range(length // size):
            pl.when(place[SLOTS + base + slot] == j)(functools.partial(block, slot, j))
        return carry

    lax.fori_loop(0, count, step, 0)
    if final:
        half = HEAD_DIM // 2
        mine = pl.ds(pl.multiple_of(place[2] * half, half), half)
        theirs = pl.ds(pl.multiple_of((1 - place[2]) * half, half), half)
        keep[:half] = dk[mine, :]
        keep[half:] = dv[mine, :]
        send[:half] = dk[theirs, :].astype(BF16)
        send[half:] = dv[theirs, :].astype(BF16)


def finish_kernel(keep, other, partial, *refs):
    received, (grad_k, grad_v, grad_weight) = refs[:-3], refs[-3:]
    half = keep.shape[0] // 2
    total = (keep[...].astype(BF16).astype(F32) + other[...].astype(F32)).astype(BF16)
    grad_k[...] = total[:half]
    grad_v[...] = total[half:]
    total = partial[...]
    for ref in received:
        total = total + ref[...].astype(F32)
    grad_weight[...] = total.astype(BF16)


def chunk(ref, c, rows):
    return ref[c] if len(ref.shape) == 3 else ref[c * rows : (c + 1) * rows, :]


def merge_kernel(first, second, *halves):
    rows = second.shape[1]
    c = 0
    for half in halves:
        for i in range(half.shape[0]):
            half[i, :rows] = chunk(first, c, rows)
            half[i, rows:] = second[c]
            c += 1


def pieces(refs, c):
    rows = refs[1].shape[1]
    return [
        jnp.concatenate([chunk(refs[i], c, rows), refs[i + 1][c]], axis=0)
        for i in range(0, len(refs), 2)
    ]


def middle_piece(place, refs, c):
    inner = (place[3] == 1) | (place[3] == 2)
    found = pieces(refs, c)
    return jnp.where(inner, found[0], found[1])


def late_piece(place, refs, i, j):
    inner = (place[3] == 1) | (place[3] == 2)
    return jnp.where(inner, refs[0][i], refs[1][j])


def attended_rows(att_own, att_other, j, rows):
    at = pl.ds(pl.multiple_of(j * rows, rows), rows)
    return jnp.concatenate([att_own[at, :], att_other[at, :]], axis=0)


def early_kernel(count, place, *refs):
    blocks, weights, (own, give) = refs[:count], refs[count:-2], refs[-2:]
    rows = own.shape[1]
    totals = None
    for c, weight in enumerate(weights):
        products = [dot(value, weight[...], 1, 0) for value in pieces(blocks, c)]
        totals = [a + b for a, b in zip(totals, products)] if totals else products
    for i, total in enumerate(totals):
        own[i] = total[:rows]
        give[i] = total[rows:].astype(BF16)


def early_term_kernel(count, place, att_own, att_other, *refs):
    blocks, outs = refs[:count], refs[count:]
    rows = blocks[1].shape[1]
    for c, out in enumerate(outs):
        total = None
        for i, value in enumerate(pieces(blocks, c)):
            product = dot(value, attended_rows(att_own, att_other, place[SLOTS + i], rows), 0, 0)
            total = product if total is None else total + product
        out[...] = total.astype(BF16)


def middle_kernel(count, place, *refs):
    middle, late, weights = refs[:4], refs[4:6], refs[6 : 6 + count]
    total, own, give = refs[6 + count :]
    rows = own.shape[1]
    value = None
    for c, weight in enumerate(weights):
        product = dot(middle_piece(place, middle, c), weight[...], 1, 0)
        value = product if value is None else value + product
    own[0] = value[:rows]
    give[0] = value[rows:].astype(BF16)
    value = None
    for i in range(late[0].shape[0]):
        product = dot(late_piece(place, late, i, i), weights[i][...], 1, 0)
        value = product if value is None else value + product
    total[...] = value


def late_kernel(chunks, place, *refs):
    count = len(chunks)
    late, weights, (early, own, give) = refs[: 2 * count], refs[2 * count : 3 * count], refs[3 * count :]
    total = early[...]
    for c, (i, j) in enumerate(chunks):
        total += dot(late_piece(place, late[2 * c : 2 * c + 2], i, j), weights[c][...], 1, 0)
    rows = own.shape[1]
    own[0] = total[:rows]
    give[0] = total[rows:].astype(BF16)


def term_kernel(c, i, j, late, spans, place, att_own, att_other, partial, *refs):
    blocks, received = refs[:late], refs[late : late + len(spans)]
    outs = refs[late + len(spans) :]
    total = partial[...].astype(F32)
    if late:
        values = [middle_piece(place, blocks[:4], c), late_piece(place, blocks[4:], i, j)]
        rows = values[0].shape[0] // 2
        slots = [place[place.shape[0] - 2], place[place.shape[0] - 1]]
        for slot, value in zip(slots, values):
            total = total + dot(value, attended_rows(att_own, att_other, slot, rows), 0, 0)
    middle = total.shape[0] // 2
    sides = [total[:middle], total[middle:]]
    for ref, span in zip(received, spans):
        for side in span:
            part = ref[...] if len(span) == 1 else ref[side * middle : (side + 1) * middle]
            sides[side] = sides[side] + part.astype(F32)
    if len(outs) == 2:
        for out, side in zip(outs, sides):
            out[...] = side.astype(out.dtype)
    else:
        outs[0][:middle] = sides[0].astype(outs[0].dtype)
        outs[0][middle:] = sides[1].astype(outs[0].dtype)


def tie(value, *others):
    return lax.optimization_barrier((value, *others))[0]


def body(queries, keys, values, grad_out, out_weight):
    dp, tensor = lax.axis_size("dp"), lax.axis_size("tensor")
    chips = dp // 2
    length, width = queries.shape
    half = keys.shape[1]
    rows = grad_out.shape[0]
    depth = out_weight.shape[0]
    index, part = lax.axis_index("dp"), lax.axis_index("tensor")
    if tensor == 4:
        inner = (part == 1) | (part == 2)
        early = 2
        slots = [0, 1, jnp.where(inner, 3, 2), jnp.where(inner, 2, 3)]
    else:
        early = tensor
        slots = list(range(tensor))
    place = jnp.stack(
        [index % 2, index // 2, part % 2, part] + [part ^ k for k in slots]
    ).astype(jnp.int32)

    def swap(value, axis, mask):
        return lax.ppermute(value, axis, [(i, i ^ mask) for i in range(lax.axis_size(axis))])

    def across(value):
        return lax.ppermute(value, "tensor", [(1, 2), (2, 1)])

    def outward(value):
        return lax.ppermute(value, "tensor", [(1, 0), (2, 3)])

    shape = jax.ShapeDtypeStruct
    order = sorted(range(chips), key=lambda s: (-s.bit_count(), s))
    half_block = shape((chips, rows, depth), BF16)
    tail = length // depth * 2 * half
    own, own_kv, give = call(
        functools.partial(prep_kernel, order),
        [half_block, shape((chips * rows + tail, depth), BF16), half_block],
        [place, keys.T, values.T, grad_out],
        0,
        scalars=1,
    )
    taken = swap(give, "dp", 1)

    near = [swap(own_kv, "tensor", 1), swap(taken, "tensor", 1)]
    weights = {0: out_weight}
    for s in reversed(order[:-1]):
        operand = tie(out_weight, near[0]) if s & (s - 1) else out_weight
        weights[s] = swap(operand, "dp", 2 * s)
    weights = [weights[s] for s in order]

    blocks = [own_kv, taken] + near
    late, second = [], []
    sizes = [1, chips - 2, 1] if chips > 2 else [1] * chips
    flops = 4 * length * depth * width // 100
    if tensor == 4:
        middle_own = across(own)
        direct = [w for s, w in zip(order, weights) if s & (s - 1) == 0]
        middle_taken = across(tie(taken, middle_own, near[0]))
        hold = []
        kv, attended, lse = call(
            forward_kernel,
            [
                shape((2, HEAD_DIM, length), BF16),
                shape((length, width), BF16),
                shape((length, HEAD_DIM), F32),
            ],
            [place, tie(queries, *hold), keys.T, values.T, near[0]],
            4 * length * length * width // 100,
            scalars=1,
        )
        in_own = outward(middle_own)
        in_taken = outward(tie(middle_taken, near[1]))
        middle = [middle_own, middle_taken, in_own, in_taken]
        att_other = swap(attended, "dp", 1)
        relay = call(
            merge_kernel,
            [shape((size, 2 * rows, depth), BF16) for size in sizes],
            near,
            400 * flops,
        )
        after = [[middle_taken, attended, *direct], [in_own, weights[0], att_other], []]
        for side in range(len(sizes)):
            second.append(across(tie(relay[side], *after[side], *second[-1:])))
    else:
        hold = []
        kv, attended, lse = call(
            forward_kernel,
            [
                shape((2, HEAD_DIM, length), BF16),
                shape((length, width), BF16),
                shape((length, HEAD_DIM), F32),
            ],
            [place, tie(queries, *hold), keys.T, values.T, near[0]],
            4 * length * length * width // 100,
            scalars=1,
        )
        att_other = swap(attended, "dp", 1)
        for k in range(2, tensor):
            blocks += [swap(own, "tensor", k), swap(taken, "tensor", k)]
    grad_own, grad_give = call(
        functools.partial(early_kernel, len(blocks)),
        [shape((early, rows, width), F32), shape((early, rows, width), BF16)],
        [place] + blocks + weights,
        300 * flops,
        scalars=1,
    )
    partials = call(
        functools.partial(early_term_kernel, len(blocks)),
        [shape((depth, width), BF16)] * chips,
        [tie(place, grad_give), attended, att_other] + blocks,
        flops,
        scalars=1,
    )
    grad_other = swap(grad_give, "dp", 1)
    def backward(first, final, base, own, other, carry):
        state = [shape((HEAD_DIM, length), F32)] * 2
        ends = [shape((2 * half, length), F32), shape((2 * half, length), BF16)]
        size = (width // HEAD_DIM * rows, length)
        scratch = [pltpu.VMEM(size, BF16)] * 2
        if final:
            scratch = [pltpu.VMEM((HEAD_DIM, length), F32)] * 2 + scratch
        return call(
            functools.partial(backward_kernel, first, final, base),
            [shape((length, width), BF16)] + (ends if final else state),
            [place, queries, kv, lse, own, other] + carry,
            flops,
            scratch=scratch,
            scalars=1,
        )

    done = backward(True, early == tensor, 0, grad_own, grad_other, [])
    if tensor == 4:
        after = [[], [in_taken, partials[0], done[1]], []]
        for side, size in enumerate(sizes):
            arrived = outward(tie(second[side], *after[side]))
            late += [(i, i, [second[side], arrived]) for i in range(size)]
    else:
        late = [(0, 0, [])] * chips
        middle = []


    received = {s: [] for s in order}

    def term(c, *others, kind=BF16):
        s = order[c]
        low, high = s & -s, 1 << s.bit_length() >> 1
        spans, extra = zip(*received[s]) if received[s] and s else ((), ())
        shapes = [(depth, width)] if low == high else [(depth // 2, width)] * 2
        found = call(
            functools.partial(term_kernel, c, *late[c][:2], len(middle + late[c][2]), spans),
            [shape(size, kind) for size in shapes],
            [tie(place, *others), attended, att_other, partials[c]]
            + middle
            + late[c][2]
            + list(extra),
            300 * flops,
            scalars=1,
        )
        if len(found) == 2:
            received[s ^ low].append(((0,), swap(found[0], "dp", 2 * low)))
            received[s ^ high].append(((1,), swap(found[1], "dp", 2 * high)))
        elif s:
            received[0].append(((0, 1), swap(found[0], "dp", 2 * s)))
        return found[0]

    terms = [term(0)]
    if tensor == 4:
        total, grad_own, grad_give = call(
            functools.partial(middle_kernel, chips),
            [
                shape((2 * rows, width), F32),
                shape((1, rows, width), F32),
                shape((1, rows, width), BF16),
            ],
            [tie(place, terms[0])] + middle + late[0][2] + weights,
            flops,
            scalars=1,
        )
        grad_other = swap(grad_give, "dp", 1)
        done = backward(False, False, early, grad_own, grad_other, list(done))
    terms += [term(c, done[1]) for c in range(1, chips - 1)]

    if tensor == 4:
        (grad_own, grad_give) = call(
            functools.partial(late_kernel, [item[:2] for item in late[sizes[0] :]]),
            [shape((1, rows, width), F32), shape((1, rows, width), BF16)],
            [tie(place, done[1])]
            + sum([item[2] for item in late[sizes[0] :]], [])
            + weights[sizes[0] :]
            + [total],
            flops,
            scalars=1,
        )
        grad_other = swap(grad_give, "dp", 1)
        done = backward(False, True, early + 1, grad_own, grad_other, list(done))
    grad_q, keep, send = done
    grad_k, grad_v, grad_weight = call(
        finish_kernel,
        [shape((half, length), BF16)] * 2 + [shape((depth, width), BF16)],
        [keep, swap(send, "tensor", 1), term(chips - 1, kind=F32)]
        + [value for _, value in received[0]],
        flops,
    )
    return grad_q, grad_k.T, grad_v.T, grad_weight


def solution(mesh):
    placed = (
        P("dp", "tensor"),
        P("dp", "tensor"),
        P("dp", "tensor"),
        P(("dp", "tensor"), None),
        P("dp", "tensor"),
    )
    return jax.shard_map(
        body,
        mesh=mesh,
        in_specs=placed,
        out_specs=(P("dp", "tensor"), P("dp", "tensor"), P("dp", "tensor"), P("dp", "tensor")),
        check_vma=False,
    )
```

```python
import functools
import math

import jax
import jax.numpy as jnp
from jax import lax
from jax.experimental import pallas as pl
from jax.experimental.pallas import tpu as pltpu
from jax.sharding import PartitionSpec as P

HEAD_DIM = 128
BLOCK = 128
VMEM_BYTES = 20 * 1024 * 1024
SLOTS = 4
SCALE = HEAD_DIM ** (-0.5)
SCALE2 = SCALE * math.log2(math.e)
VMEM = pl.BlockSpec(memory_space=pltpu.VMEM)
SMEM = pl.BlockSpec(memory_space=pltpu.SMEM)
F32 = jnp.float32
BF16 = jnp.bfloat16


def call(kernel, outs, args, flops, scratch=(), scalars=0):
    size = sum(math.prod(a.shape) * a.dtype.itemsize for a in list(args) + list(outs))
    return pl.pallas_call(
        kernel,
        out_shape=tuple(outs),
        in_specs=[SMEM] * scalars + [VMEM] * (len(args) - scalars),
        out_specs=tuple([VMEM] * len(outs)),
        scratch_shapes=list(scratch),
        cost_estimate=pl.CostEstimate(flops=flops, bytes_accessed=size // 100, transcendentals=0),
        compiler_params=pltpu.CompilerParams(vmem_limit_bytes=VMEM_BYTES),
    )(*args)


def dot(a, b, ca, cb):
    return lax.dot_general(a, b, (((ca,), (cb,)), ((), ())), preferred_element_type=F32)


def prep_kernel(order, place, keys, values, grad, own, own_kv, give):
    core, chip = place[0], place[1]
    chips, rows, width = own.shape
    half, length = keys.shape
    for k, s in enumerate(order):
        first = (chip ^ s) * 2
        own[k] = grad[:, pl.ds(pl.multiple_of((first + core) * width, 128), width)]
        own_kv[k * rows : (k + 1) * rows, :] = own[k]
        give[k] = grad[:, pl.ds(pl.multiple_of((first + 1 - core) * width, 128), width)]
    for i in range(length // width):
        at = chips * rows + i * 2 * half
        own_kv[at : at + half, :] = keys[:, i * width : (i + 1) * width]
        own_kv[at + half : at + 2 * half, :] = values[:, i * width : (i + 1) * width]


def forward_kernel(place, queries, keys, values, near, kv, attended, lse):
    parity = place[2]
    half, length = keys.shape
    depth = near.shape[1]
    mine = pl.multiple_of(parity * half, half)
    theirs = pl.multiple_of((1 - parity) * half, half)
    tail = near.shape[0] - length // depth * 2 * half
    for part, ref in enumerate((keys, values)):
        kv[part, pl.ds(mine, half), :] = ref[...]
        for i in range(length // depth):
            at = tail + (2 * i + part) * half
            kv[part, pl.ds(theirs, half), i * depth : (i + 1) * depth] = near[at : at + half, :]
    length, width = queries.shape
    row = lax.broadcasted_iota(jnp.int32, (BLOCK, BLOCK), 0)
    col = lax.broadcasted_iota(jnp.int32, (BLOCK, BLOCK), 1)
    for i in range(length // BLOCK):
        rows = pl.ds(i * BLOCK, BLOCK)
        keys = (i + 1) * BLOCK
        stats = []
        for h in range(width // HEAD_DIM):
            cols = pl.ds(h * HEAD_DIM, HEAD_DIM)
            scores = dot(queries[rows, cols], kv[0, :, :keys], 1, 0) * SCALE2
            last = jnp.where(col <= row, scores[:, keys - BLOCK :], -jnp.inf)
            top = jnp.max(last, axis=1, keepdims=True)
            if i:
                top = jnp.maximum(top, jnp.max(scores[:, : keys - BLOCK], axis=1, keepdims=True))
            powers = jnp.exp2(last - top)
            total = jnp.sum(powers, axis=1, keepdims=True)
            if i:
                early = jnp.exp2(scores[:, : keys - BLOCK] - top)
                total = total + jnp.sum(early, axis=1, keepdims=True)
                powers = jnp.concatenate([early, powers], axis=1)
            probs = (powers / total).astype(BF16)
            attended[rows, cols] = dot(probs, kv[1, :, :keys], 1, 1).astype(BF16)
            stats.append(jnp.broadcast_to(top + jnp.log2(total), (BLOCK, HEAD_DIM)))
        lane = lax.broadcasted_iota(jnp.int32, (BLOCK, HEAD_DIM), 1)
        packed = stats[0]
        for h, stat in enumerate(stats):
            packed = jnp.where(lane == h, stat, packed)
        lse[rows, :] = packed


def backward_kernel(first, final, base, place, queries, kv, lse, grad_own, grad_other, *refs):
    if not first:
        early_q, early_k, early_v = refs[:3]
        refs = refs[3:]
    if final:
        grad_q, keep, send, dk, dv = refs
    else:
        grad_q, dk, dv = refs
    if first:
        dk[...] = jnp.zeros_like(dk)
        dv[...] = jnp.zeros_like(dv)
    else:
        grad_q[...] = early_q[...]
        dk[...] = early_k[...]
        dv[...] = early_v[...]
    length, width = queries.shape
    heads = width // HEAD_DIM
    count, size, _ = grad_own.shape
    row = lax.broadcasted_iota(jnp.int32, (size, BLOCK), 0)
    col = lax.broadcasted_iota(jnp.int32, (size, BLOCK), 1)

    def block(slot, j):
        rows = pl.ds(j * size, size)
        keys = -(-(j + 1) * size // BLOCK) * BLOCK
        early = keys - BLOCK
        columns = [pl.ds(h * HEAD_DIM, HEAD_DIM) for h in range(heads)]
        lhs = [queries[rows, cols] for cols in columns]
        grads = [
            (grad_own[slot, :, cols] + grad_other[slot, :, cols].astype(F32)).astype(BF16)
            for cols in columns
        ]
        scores = [dot(value, kv[0, :, :keys], 1, 0) for value in lhs]
        dprobs = [dot(value, kv[1, :, :keys], 1, 0) for value in grads]
        halves, dscores = [], []
        for h in range(heads):
            probs = jnp.exp2(scores[h] * SCALE2 - lse[rows, h : h + 1])
            last = jnp.where(col + early <= row + j * size, probs[:, early:], 0.0)
            probs = jnp.concatenate([probs[:, :early], last], axis=1) if early else last
            delta = jnp.sum(probs * dprobs[h], axis=1, keepdims=True)
            dscores.append((probs * (dprobs[h] - delta) * SCALE).astype(BF16))
            halves.append(probs.astype(BF16))
        for h, cols in enumerate(columns):
            grad_q[rows, cols] = dot(dscores[h], kv[0, :, :keys], 1, 1).astype(BF16)
        dk[:, :keys] += dot(jnp.concatenate(lhs, axis=0), jnp.concatenate(dscores, axis=0), 0, 0)
        dv[:, :keys] += dot(jnp.concatenate(grads, axis=0), jnp.concatenate(halves, axis=0), 0, 0)

    def step(slot, carry):
        for j in range(length // size):
            pl.when(place[SLOTS + base + slot] == j)(functools.partial(block, slot, j))
        return carry

    lax.fori_loop(0, count, step, 0)
    if final:
        half = HEAD_DIM // 2
        mine = pl.ds(pl.multiple_of(place[2] * half, half), half)
        theirs = pl.ds(pl.multiple_of((1 - place[2]) * half, half), half)
        keep[:half] = dk[mine, :]
        keep[half:] = dv[mine, :]
        send[:half] = dk[theirs, :].astype(BF16)
        send[half:] = dv[theirs, :].astype(BF16)


def finish_kernel(keep, other, partial, *refs):
    received, (grad_k, grad_v, grad_weight) = refs[:-3], refs[-3:]
    half = keep.shape[0] // 2
    total = (keep[...].astype(BF16).astype(F32) + other[...].astype(F32)).astype(BF16)
    grad_k[...] = total[:half]
    grad_v[...] = total[half:]
    total = partial[...]
    for ref in received:
        total = total + ref[...].astype(F32)
    grad_weight[...] = total.astype(BF16)


def chunk(ref, c, rows):
    return ref[c] if len(ref.shape) == 3 else ref[c * rows : (c + 1) * rows, :]


def merge_kernel(first, second, *halves):
    rows = second.shape[1]
    c = 0
    for half in halves:
        for i in range(half.shape[0]):
            half[i, :rows] = chunk(first, c, rows)
            half[i, rows:] = second[c]
            c += 1


def pieces(refs, c):
    rows = refs[1].shape[1]
    return [
        jnp.concatenate([chunk(refs[i], c, rows), refs[i + 1][c]], axis=0)
        for i in range(0, len(refs), 2)
    ]


def middle_piece(place, refs, c):
    inner = (place[3] == 1) | (place[3] == 2)
    found = pieces(refs, c)
    return jnp.where(inner, found[0], found[1])


def late_piece(place, refs, i, j):
    inner = (place[3] == 1) | (place[3] == 2)
    return jnp.where(inner, refs[0][i], refs[1][j])


def attended_rows(att_own, att_other, j, rows):
    at = pl.ds(pl.multiple_of(j * rows, rows), rows)
    return jnp.concatenate([att_own[at, :], att_other[at, :]], axis=0)


def early_kernel(count, place, *refs):
    blocks, weights, (own, give) = refs[:count], refs[count:-2], refs[-2:]
    rows = own.shape[1]
    totals = None
    for c, weight in enumerate(weights):
        products = [dot(value, weight[...], 1, 0) for value in pieces(blocks, c)]
        totals = [a + b for a, b in zip(totals, products)] if totals else products
    for i, total in enumerate(totals):
        own[i] = total[:rows]
        give[i] = total[rows:].astype(BF16)


def early_term_kernel(count, place, att_own, att_other, *refs):
    blocks, outs = refs[:count], refs[count:]
    rows = blocks[1].shape[1]
    for c, out in enumerate(outs):
        total = None
        for i, value in enumerate(pieces(blocks, c)):
            product = dot(value, attended_rows(att_own, att_other, place[SLOTS + i], rows), 0, 0)
            total = product if total is None else total + product
        out[...] = total.astype(BF16)


def middle_kernel(count, place, *refs):
    middle, late, weights, out = refs[:4], refs[4:6], refs[6 : 6 + count], refs[-1]
    total = None
    for c, weight in enumerate(weights):
        product = dot(middle_piece(place, middle, c), weight[...], 1, 0)
        total = product if total is None else total + product
    out[0] = total
    total = None
    for i in range(late[0].shape[0]):
        product = dot(late_piece(place, late, i, i), weights[i][...], 1, 0)
        total = product if total is None else total + product
    out[1] = total


def late_kernel(chunks, place, *refs):
    count = len(chunks)
    late, weights = refs[: 2 * count], refs[2 * count : 3 * count]
    early, own, give = refs[3 * count :]
    total = early[1]
    for c, (i, j) in enumerate(chunks):
        total += dot(late_piece(place, late[2 * c : 2 * c + 2], i, j), weights[c][...], 1, 0)
    rows = own.shape[1]
    for q, value in enumerate((early[0], total)):
        own[q] = value[:rows]
        give[q] = value[rows:].astype(BF16)


def term_kernel(c, i, j, late, spans, place, att_own, att_other, partial, *refs):
    blocks, received = refs[:late], refs[late : late + len(spans)]
    outs = refs[late + len(spans) :]
    total = partial[...].astype(F32)
    if late:
        values = [middle_piece(place, blocks[:4], c), late_piece(place, blocks[4:], i, j)]
        rows = values[0].shape[0] // 2
        slots = [place[place.shape[0] - 2], place[place.shape[0] - 1]]
        for slot, value in zip(slots, values):
            total = total + dot(value, attended_rows(att_own, att_other, slot, rows), 0, 0)
    middle = total.shape[0] // 2
    sides = [total[:middle], total[middle:]]
    for ref, span in zip(received, spans):
        for side in span:
            part = ref[...] if len(span) == 1 else ref[side * middle : (side + 1) * middle]
            sides[side] = sides[side] + part.astype(F32)
    if len(outs) == 2:
        for out, side in zip(outs, sides):
            out[...] = side.astype(out.dtype)
    else:
        outs[0][:middle] = sides[0].astype(outs[0].dtype)
        outs[0][middle:] = sides[1].astype(outs[0].dtype)


def tie(value, *others):
    return lax.optimization_barrier((value, *others))[0]


def body(queries, keys, values, grad_out, out_weight):
    dp, tensor = lax.axis_size("dp"), lax.axis_size("tensor")
    chips = dp // 2
    length, width = queries.shape
    half = keys.shape[1]
    rows = grad_out.shape[0]
    depth = out_weight.shape[0]
    index, part = lax.axis_index("dp"), lax.axis_index("tensor")
    if tensor == 4:
        inner = (part == 1) | (part == 2)
        early = 2
        slots = [0, 1, jnp.where(inner, 3, 2), jnp.where(inner, 2, 3)]
    else:
        early = tensor
        slots = list(range(tensor))
    place = jnp.stack(
        [index % 2, index // 2, part % 2, part] + [part ^ k for k in slots]
    ).astype(jnp.int32)

    def swap(value, axis, mask):
        return lax.ppermute(value, axis, [(i, i ^ mask) for i in range(lax.axis_size(axis))])

    def across(value):
        return lax.ppermute(value, "tensor", [(1, 2), (2, 1)])

    def outward(value):
        return lax.ppermute(value, "tensor", [(1, 0), (2, 3)])

    shape = jax.ShapeDtypeStruct
    order = sorted(range(chips), key=lambda s: (-s.bit_count(), s))
    half_block = shape((chips, rows, depth), BF16)
    tail = length // depth * 2 * half
    own, own_kv, give = call(
        functools.partial(prep_kernel, order),
        [half_block, shape((chips * rows + tail, depth), BF16), half_block],
        [place, keys.T, values.T, grad_out],
        0,
        scalars=1,
    )
    taken = swap(give, "dp", 1)

    near = [swap(own_kv, "tensor", 1), swap(taken, "tensor", 1)]
    weights = {0: out_weight}
    for s in reversed(order[:-1]):
        operand = tie(out_weight, near[0]) if s & (s - 1) else out_weight
        weights[s] = swap(operand, "dp", 2 * s)
    weights = [weights[s] for s in order]

    blocks = [own_kv, taken] + near
    late, second = [], []
    sizes = [1, chips - 2, 1] if chips > 2 else [1] * chips
    flops = 4 * length * depth * width // 100
    if tensor == 4:
        middle_own = across(own)
        direct = [w for s, w in zip(order, weights) if s & (s - 1) == 0]
        middle_taken = across(tie(taken, middle_own, near[0]))
        hold = []
        kv, attended, lse = call(
            forward_kernel,
            [
                shape((2, HEAD_DIM, length), BF16),
                shape((length, width), BF16),
                shape((length, HEAD_DIM), F32),
            ],
            [place, tie(queries, *hold), keys.T, values.T, near[0]],
            4 * length * length * width // 100,
            scalars=1,
        )
        in_own = outward(middle_own)
        in_taken = outward(tie(middle_taken, near[1]))
        middle = [middle_own, middle_taken, in_own, in_taken]
        att_other = swap(attended, "dp", 1)
        relay = call(
            merge_kernel,
            [shape((size, 2 * rows, depth), BF16) for size in sizes],
            near,
            400 * flops,
        )
        after = [[middle_taken, attended, *direct], [in_own, weights[0], att_other], []]
        for side in range(len(sizes)):
            second.append(across(tie(relay[side], *after[side], *second[-1:])))
    else:
        hold = []
        kv, attended, lse = call(
            forward_kernel,
            [
                shape((2, HEAD_DIM, length), BF16),
                shape((length, width), BF16),
                shape((length, HEAD_DIM), F32),
            ],
            [place, tie(queries, *hold), keys.T, values.T, near[0]],
            4 * length * length * width // 100,
            scalars=1,
        )
        att_other = swap(attended, "dp", 1)
        for k in range(2, tensor):
            blocks += [swap(own, "tensor", k), swap(taken, "tensor", k)]
    grad_own, grad_give = call(
        functools.partial(early_kernel, len(blocks)),
        [shape((early, rows, width), F32), shape((early, rows, width), BF16)],
        [place] + blocks + weights,
        300 * flops,
        scalars=1,
    )
    partials = call(
        functools.partial(early_term_kernel, len(blocks)),
        [shape((depth, width), BF16)] * chips,
        [tie(place, grad_give), attended, att_other] + blocks,
        flops,
        scalars=1,
    )
    grad_other = swap(grad_give, "dp", 1)
    def backward(first, final, base, own, other, carry):
        state = [shape((HEAD_DIM, length), F32)] * 2
        ends = [shape((2 * half, length), F32), shape((2 * half, length), BF16)]
        scratch = [pltpu.VMEM((HEAD_DIM, length), F32)] * 2 if final else []
        return call(
            functools.partial(backward_kernel, first, final, base),
            [shape((length, width), BF16)] + (ends if final else state),
            [place, queries, kv, lse, own, other] + carry,
            flops,
            scratch=scratch,
            scalars=1,
        )

    done = backward(True, early == tensor, 0, grad_own, grad_other, [])
    if tensor == 4:
        after = [[], [in_taken, partials[0], done[1]], []]
        for side, size in enumerate(sizes):
            arrived = outward(tie(second[side], *after[side]))
            late += [(i, i, [second[side], arrived]) for i in range(size)]
    else:
        late = [(0, 0, [])] * chips
        middle = []


    received = {s: [] for s in order}

    def term(c, *others, kind=BF16):
        s = order[c]
        low, high = s & -s, 1 << s.bit_length() >> 1
        spans, extra = zip(*received[s]) if received[s] and s else ((), ())
        shapes = [(depth, width)] if low == high else [(depth // 2, width)] * 2
        found = call(
            functools.partial(term_kernel, c, *late[c][:2], len(middle + late[c][2]), spans),
            [shape(size, kind) for size in shapes],
            [tie(place, *others), attended, att_other, partials[c]]
            + middle
            + late[c][2]
            + list(extra),
            300 * flops,
            scalars=1,
        )
        if len(found) == 2:
            received[s ^ low].append(((0,), swap(found[0], "dp", 2 * low)))
            received[s ^ high].append(((1,), swap(found[1], "dp", 2 * high)))
        elif s:
            received[0].append(((0, 1), swap(found[0], "dp", 2 * s)))
        return found[0]

    terms = [term(0)]
    total = place
    if tensor == 4:
        (total,) = call(
            functools.partial(middle_kernel, chips),
            [shape((2, 2 * rows, width), F32)],
            [tie(place, terms[0])] + middle + late[0][2] + weights,
            flops,
            scalars=1,
        )
    terms += [term(c, total) for c in range(1, chips - 1)]

    if tensor == 4:
        ends = late[sizes[0] :]
        grad_own, grad_give = call(
            functools.partial(late_kernel, [item[:2] for item in ends]),
            [shape((2, rows, width), F32), shape((2, rows, width), BF16)],
            [place] + sum([item[2] for item in ends], []) + weights[sizes[0] :] + [total],
            flops,
            scalars=1,
        )
        grad_other = swap(grad_give, "dp", 1)
        done = backward(False, True, early, grad_own, grad_other, list(done))
    grad_q, keep, send = done
    grad_k, grad_v, grad_weight = call(
        finish_kernel,
        [shape((half, length), BF16)] * 2 + [shape((depth, width), BF16)],
        [keep, swap(send, "tensor", 1), term(chips - 1, kind=F32)]
        + [value for _, value in received[0]],
        flops,
    )
    return grad_q, grad_k.T, grad_v.T, grad_weight


def solution(mesh):
    placed = (
        P("dp", "tensor"),
        P("dp", "tensor"),
        P("dp", "tensor"),
        P(("dp", "tensor"), None),
        P("dp", "tensor"),
    )
    return jax.shard_map(
        body,
        mesh=mesh,
        in_specs=placed,
        out_specs=(P("dp", "tensor"), P("dp", "tensor"), P("dp", "tensor"), P("dp", "tensor")),
        check_vma=False,
    )
```

```python
import functools
import math

import jax
import jax.numpy as jnp
from jax import lax
from jax.experimental import pallas as pl
from jax.experimental.pallas import tpu as pltpu
from jax.sharding import PartitionSpec as P

HEAD_DIM = 128
BLOCK = 128
VMEM_BYTES = 20 * 1024 * 1024
SLOTS = 4
SCALE = HEAD_DIM ** (-0.5)
SCALE2 = SCALE * math.log2(math.e)
VMEM = pl.BlockSpec(memory_space=pltpu.VMEM)
SMEM = pl.BlockSpec(memory_space=pltpu.SMEM)
F32 = jnp.float32
BF16 = jnp.bfloat16


def call(kernel, outs, args, flops, scratch=(), scalars=0):
    size = sum(math.prod(a.shape) * a.dtype.itemsize for a in list(args) + list(outs))
    return pl.pallas_call(
        kernel,
        out_shape=tuple(outs),
        in_specs=[SMEM] * scalars + [VMEM] * (len(args) - scalars),
        out_specs=tuple([VMEM] * len(outs)),
        scratch_shapes=list(scratch),
        cost_estimate=pl.CostEstimate(flops=flops, bytes_accessed=size // 100, transcendentals=0),
        compiler_params=pltpu.CompilerParams(vmem_limit_bytes=VMEM_BYTES),
    )(*args)


def dot(a, b, ca, cb):
    return lax.dot_general(a, b, (((ca,), (cb,)), ((), ())), preferred_element_type=F32)


def prep_kernel(order, place, keys, values, grad, own, own_kv, give):
    core, chip = place[0], place[1]
    chips, rows, width = own.shape
    half, length = keys.shape
    for k, s in enumerate(order):
        first = (chip ^ s) * 2
        own[k] = grad[:, pl.ds(pl.multiple_of((first + core) * width, 128), width)]
        own_kv[k * rows : (k + 1) * rows, :] = own[k]
        give[k] = grad[:, pl.ds(pl.multiple_of((first + 1 - core) * width, 128), width)]
    for i in range(length // width):
        at = chips * rows + i * 2 * half
        own_kv[at : at + half, :] = keys[:, i * width : (i + 1) * width]
        own_kv[at + half : at + 2 * half, :] = values[:, i * width : (i + 1) * width]


def forward_kernel(place, queries, keys, values, near, kv, attended, lse):
    parity = place[2]
    half, length = keys.shape
    depth = near.shape[1]
    mine = pl.multiple_of(parity * half, half)
    theirs = pl.multiple_of((1 - parity) * half, half)
    tail = near.shape[0] - length // depth * 2 * half
    for part, ref in enumerate((keys, values)):
        kv[part, pl.ds(mine, half), :] = ref[...]
        for i in range(length // depth):
            at = tail + (2 * i + part) * half
            kv[part, pl.ds(theirs, half), i * depth : (i + 1) * depth] = near[at : at + half, :]
    length, width = queries.shape
    row = lax.broadcasted_iota(jnp.int32, (BLOCK, BLOCK), 0)
    col = lax.broadcasted_iota(jnp.int32, (BLOCK, BLOCK), 1)
    for i in range(length // BLOCK):
        rows = pl.ds(i * BLOCK, BLOCK)
        keys = (i + 1) * BLOCK
        stats = []
        for h in range(width // HEAD_DIM):
            cols = pl.ds(h * HEAD_DIM, HEAD_DIM)
            scores = dot(queries[rows, cols], kv[0, :, :keys], 1, 0) * SCALE2
            last = jnp.where(col <= row, scores[:, keys - BLOCK :], -jnp.inf)
            top = jnp.max(last, axis=1, keepdims=True)
            if i:
                top = jnp.maximum(top, jnp.max(scores[:, : keys - BLOCK], axis=1, keepdims=True))
            powers = jnp.exp2(last - top)
            total = jnp.sum(powers, axis=1, keepdims=True)
            if i:
                early = jnp.exp2(scores[:, : keys - BLOCK] - top)
                total = total + jnp.sum(early, axis=1, keepdims=True)
                powers = jnp.concatenate([early, powers], axis=1)
            probs = (powers / total).astype(BF16)
            attended[rows, cols] = dot(probs, kv[1, :, :keys], 1, 1).astype(BF16)
            stats.append(jnp.broadcast_to(top + jnp.log2(total), (BLOCK, HEAD_DIM)))
        lane = lax.broadcasted_iota(jnp.int32, (BLOCK, HEAD_DIM), 1)
        packed = stats[0]
        for h, stat in enumerate(stats):
            packed = jnp.where(lane == h, stat, packed)
        lse[rows, :] = packed


def backward_kernel(first, final, base, place, queries, kv, lse, grad_own, grad_other, *refs):
    if not first:
        early_q, early_k, early_v = refs[:3]
        refs = refs[3:]
    if final:
        grad_q, keep, send, dk, dv = refs
    else:
        grad_q, dk, dv = refs
    if first:
        dk[...] = jnp.zeros_like(dk)
        dv[...] = jnp.zeros_like(dv)
    else:
        grad_q[...] = early_q[...]
        dk[...] = early_k[...]
        dv[...] = early_v[...]
    length, width = queries.shape
    heads = width // HEAD_DIM
    count, size, _ = grad_own.shape
    row = lax.broadcasted_iota(jnp.int32, (size, BLOCK), 0)
    col = lax.broadcasted_iota(jnp.int32, (size, BLOCK), 1)

    def block(slot, j):
        rows = pl.ds(j * size, size)
        keys = -(-(j + 1) * size // BLOCK) * BLOCK
        early = keys - BLOCK
        columns = [pl.ds(h * HEAD_DIM, HEAD_DIM) for h in range(heads)]
        lhs = [queries[rows, cols] for cols in columns]
        grads = [
            (grad_own[slot, :, cols] + grad_other[slot, :, cols].astype(F32)).astype(BF16)
            for cols in columns
        ]
        scores = [dot(value, kv[0, :, :keys], 1, 0) for value in lhs]
        dprobs = [dot(value, kv[1, :, :keys], 1, 0) for value in grads]
        halves, dscores = [], []
        for h in range(heads):
            probs = jnp.exp2(scores[h] * SCALE2 - lse[rows, h : h + 1])
            last = jnp.where(col + early <= row + j * size, probs[:, early:], 0.0)
            probs = jnp.concatenate([probs[:, :early], last], axis=1) if early else last
            delta = jnp.sum(probs * dprobs[h], axis=1, keepdims=True)
            dscores.append((probs * (dprobs[h] - delta) * SCALE).astype(BF16))
            halves.append(probs.astype(BF16))
        for h, cols in enumerate(columns):
            grad_q[rows, cols] = dot(dscores[h], kv[0, :, :keys], 1, 1).astype(BF16)
        dk[:, :keys] += dot(jnp.concatenate(lhs, axis=0), jnp.concatenate(dscores, axis=0), 0, 0)
        dv[:, :keys] += dot(jnp.concatenate(grads, axis=0), jnp.concatenate(halves, axis=0), 0, 0)

    def step(slot, carry):
        for j in range(length // size):
            pl.when(place[SLOTS + base + slot] == j)(functools.partial(block, slot, j))
        return carry

    lax.fori_loop(0, count, step, 0)
    if final:
        half = HEAD_DIM // 2
        mine = pl.ds(pl.multiple_of(place[2] * half, half), half)
        theirs = pl.ds(pl.multiple_of((1 - place[2]) * half, half), half)
        keep[:half] = dk[mine, :]
        keep[half:] = dv[mine, :]
        send[:half] = dk[theirs, :].astype(BF16)
        send[half:] = dv[theirs, :].astype(BF16)


def finish_kernel(keep, other, partial, *refs):
    received, (grad_k, grad_v, grad_weight) = refs[:-3], refs[-3:]
    half = keep.shape[0] // 2
    total = (keep[...].astype(BF16).astype(F32) + other[...].astype(F32)).astype(BF16)
    grad_k[...] = total[:half]
    grad_v[...] = total[half:]
    total = partial[...]
    for ref in received:
        total = total + ref[...].astype(F32)
    grad_weight[...] = total.astype(BF16)


def chunk(ref, c, rows):
    return ref[c] if len(ref.shape) == 3 else ref[c * rows : (c + 1) * rows, :]


def merge_kernel(first, second, *halves):
    rows = second.shape[1]
    c = 0
    for half in halves:
        for i in range(half.shape[0]):
            half[i, :rows] = chunk(first, c, rows)
            half[i, rows:] = second[c]
            c += 1


def pieces(refs, c):
    rows = refs[1].shape[1]
    return [
        jnp.concatenate([chunk(refs[i], c, rows), refs[i + 1][c]], axis=0)
        for i in range(0, len(refs), 2)
    ]


def middle_piece(place, refs, c):
    inner = (place[3] == 1) | (place[3] == 2)
    found = pieces(refs, c)
    return jnp.where(inner, found[0], found[1])


def late_piece(place, refs, i, j):
    inner = (place[3] == 1) | (place[3] == 2)
    return jnp.where(inner, refs[0][i], refs[1][j])


def attended_rows(att_own, att_other, j, rows):
    at = pl.ds(pl.multiple_of(j * rows, rows), rows)
    return jnp.concatenate([att_own[at, :], att_other[at, :]], axis=0)


def early_kernel(count, place, *refs):
    blocks, weights, (own, give) = refs[:count], refs[count:-2], refs[-2:]
    rows = own.shape[1]
    totals = None
    for c, weight in enumerate(weights):
        products = [dot(value, weight[...], 1, 0) for value in pieces(blocks, c)]
        totals = [a + b for a, b in zip(totals, products)] if totals else products
    for i, total in enumerate(totals):
        own[i] = total[:rows]
        give[i] = total[rows:].astype(BF16)


def early_term_kernel(count, place, att_own, att_other, *refs):
    blocks, outs = refs[:count], refs[count:]
    rows = blocks[1].shape[1]
    for c, out in enumerate(outs):
        total = None
        for i, value in enumerate(pieces(blocks, c)):
            product = dot(value, attended_rows(att_own, att_other, place[SLOTS + i], rows), 0, 0)
            total = product if total is None else total + product
        out[...] = total.astype(BF16)


def middle_kernel(count, place, *refs):
    middle, late, weights, out = refs[:4], refs[4:6], refs[6 : 6 + count], refs[-1]
    total = None
    for c, weight in enumerate(weights):
        product = dot(middle_piece(place, middle, c), weight[...], 1, 0)
        total = product if total is None else total + product
    out[0] = total
    total = None
    for i in range(late[0].shape[0]):
        product = dot(late_piece(place, late, i, i), weights[i][...], 1, 0)
        total = product if total is None else total + product
    out[1] = total


def late_kernel(chunks, place, *refs):
    count = len(chunks)
    late, weights = refs[: 2 * count], refs[2 * count : 3 * count]
    early, own, give = refs[3 * count :]
    total = early[1]
    for c, (i, j) in enumerate(chunks):
        total += dot(late_piece(place, late[2 * c : 2 * c + 2], i, j), weights[c][...], 1, 0)
    rows = own.shape[1]
    for q, value in enumerate((early[0], total)):
        own[q] = value[:rows]
        give[q] = value[rows:].astype(BF16)


def term_kernel(c, i, j, late, count, place, att_own, att_other, partial, *refs):
    blocks, received, outs = refs[:late], refs[late : late + count], refs[late + count :]
    total = partial[...].astype(F32)
    if late:
        values = [middle_piece(place, blocks[:4], c), late_piece(place, blocks[4:], i, j)]
        rows = values[0].shape[0] // 2
        slots = [place[place.shape[0] - 2], place[place.shape[0] - 1]]
        for slot, value in zip(slots, values):
            total = total + dot(value, attended_rows(att_own, att_other, slot, rows), 0, 0)
    for ref in received:
        total = total + ref[...].astype(F32)
    outs[0][...] = total.astype(outs[0].dtype)


def tie(value, *others):
    return lax.optimization_barrier((value, *others))[0]


def body(queries, keys, values, grad_out, out_weight):
    dp, tensor = lax.axis_size("dp"), lax.axis_size("tensor")
    chips = dp // 2
    length, width = queries.shape
    half = keys.shape[1]
    rows = grad_out.shape[0]
    depth = out_weight.shape[0]
    index, part = lax.axis_index("dp"), lax.axis_index("tensor")
    if tensor == 4:
        inner = (part == 1) | (part == 2)
        early = 2
        slots = [0, 1, jnp.where(inner, 3, 2), jnp.where(inner, 2, 3)]
    else:
        early = tensor
        slots = list(range(tensor))
    place = jnp.stack(
        [index % 2, index // 2, part % 2, part] + [part ^ k for k in slots]
    ).astype(jnp.int32)

    def swap(value, axis, mask):
        return lax.ppermute(value, axis, [(i, i ^ mask) for i in range(lax.axis_size(axis))])

    def across(value):
        return lax.ppermute(value, "tensor", [(1, 2), (2, 1)])

    def outward(value):
        return lax.ppermute(value, "tensor", [(1, 0), (2, 3)])

    shape = jax.ShapeDtypeStruct
    order = sorted(range(chips), key=lambda s: (-s.bit_count(), s))
    half_block = shape((chips, rows, depth), BF16)
    tail = length // depth * 2 * half
    own, own_kv, give = call(
        functools.partial(prep_kernel, order),
        [half_block, shape((chips * rows + tail, depth), BF16), half_block],
        [place, keys.T, values.T, grad_out],
        0,
        scalars=1,
    )
    taken = swap(give, "dp", 1)

    near = [swap(own_kv, "tensor", 1), swap(taken, "tensor", 1)]
    weights = {0: out_weight}
    for s in reversed(order[:-1]):
        operand = tie(out_weight, near[0]) if s > 1 else out_weight
        weights[s] = swap(operand, "dp", 2 * s)
    weights = [weights[s] for s in order]

    blocks = [own_kv, taken] + near
    late, second = [], []
    sizes = [1, chips - 2, 1] if chips > 2 else [1] * chips
    flops = 4 * length * depth * width // 100
    if tensor == 4:
        middle_own = across(own)
        direct = [w for s, w in zip(order, weights) if s < 2]
        middle_taken = across(taken)
        hold = []
        kv, attended, lse = call(
            forward_kernel,
            [
                shape((2, HEAD_DIM, length), BF16),
                shape((length, width), BF16),
                shape((length, HEAD_DIM), F32),
            ],
            [place, tie(queries, *hold), keys.T, values.T, near[0]],
            4 * length * length * width // 100,
            scalars=1,
        )
        in_own = outward(middle_own)
        in_taken = outward(tie(middle_taken, near[1]))
        middle = [middle_own, middle_taken, in_own, in_taken]
        att_other = swap(attended, "dp", 1)
        relay = call(
            merge_kernel,
            [shape((size, 2 * rows, depth), BF16) for size in sizes],
            near,
            400 * flops,
        )
        after = [[middle_taken, attended, *weights[1:]], [in_own, *weights, att_other], []]
        for side in range(len(sizes)):
            second.append(across(tie(relay[side], *after[side], *second[-1:])))
    else:
        hold = []
        kv, attended, lse = call(
            forward_kernel,
            [
                shape((2, HEAD_DIM, length), BF16),
                shape((length, width), BF16),
                shape((length, HEAD_DIM), F32),
            ],
            [place, tie(queries, *hold), keys.T, values.T, near[0]],
            4 * length * length * width // 100,
            scalars=1,
        )
        att_other = swap(attended, "dp", 1)
        for k in range(2, tensor):
            blocks += [swap(own, "tensor", k), swap(taken, "tensor", k)]
    grad_own, grad_give = call(
        functools.partial(early_kernel, len(blocks)),
        [shape((early, rows, width), F32), shape((early, rows, width), BF16)],
        [place] + blocks + weights,
        300 * flops,
        scalars=1,
    )
    partials = call(
        functools.partial(early_term_kernel, len(blocks)),
        [shape((depth, width), BF16)] * chips,
        [tie(place, grad_give), attended, att_other] + blocks,
        flops,
        scalars=1,
    )
    grad_other = swap(grad_give, "dp", 1)
    def backward(first, final, base, own, other, carry):
        state = [shape((HEAD_DIM, length), F32)] * 2
        ends = [shape((2 * half, length), F32), shape((2 * half, length), BF16)]
        scratch = [pltpu.VMEM((HEAD_DIM, length), F32)] * 2 if final else []
        return call(
            functools.partial(backward_kernel, first, final, base),
            [shape((length, width), BF16)] + (ends if final else state),
            [place, queries, kv, lse, own, other] + carry,
            flops,
            scratch=scratch,
            scalars=1,
        )

    done = backward(True, early == tensor, 0, grad_own, grad_other, [])
    if tensor == 4:
        after = [[], [in_taken, partials[0], done[1]], []]
        for side, size in enumerate(sizes):
            arrived = outward(tie(second[side], *after[side]))
            late += [(i, i, [second[side], arrived]) for i in range(size)]
    else:
        late = [(0, 0, [])] * chips
        middle = []


    received = {s: [] for s in order}

    def term(c, *others, kind=BF16):
        s = order[c]
        extra = received[s] if s else []
        (found,) = call(
            functools.partial(
                term_kernel, c, *late[c][:2], len(middle + late[c][2]), len(extra)
            ),
            [shape((depth, width), kind)],
            [tie(place, *others), attended, att_other, partials[c]]
            + middle
            + late[c][2]
            + extra,
            300 * flops,
            scalars=1,
        )
        if s:
            low = s & -s
            received[s ^ low].append(swap(found, "dp", 2 * low))
        return found

    terms = [term(0)]
    total = place
    if tensor == 4:
        (total,) = call(
            functools.partial(middle_kernel, chips),
            [shape((2, 2 * rows, width), F32)],
            [tie(place, terms[0])] + middle + late[0][2] + weights,
            flops,
            scalars=1,
        )
    terms += [term(c, total) for c in range(1, chips - 1)]

    if tensor == 4:
        ends = late[sizes[0] :]
        grad_own, grad_give = call(
            functools.partial(late_kernel, [item[:2] for item in ends]),
            [shape((2, rows, width), F32), shape((2, rows, width), BF16)],
            [place] + sum([item[2] for item in ends], []) + weights[sizes[0] :] + [total],
            flops,
            scalars=1,
        )
        grad_other = swap(grad_give, "dp", 1)
        done = backward(False, True, early, grad_own, grad_other, list(done))
    grad_q, keep, send = done
    grad_k, grad_v, grad_weight = call(
        finish_kernel,
        [shape((half, length), BF16)] * 2 + [shape((depth, width), BF16)],
        [keep, swap(send, "tensor", 1), term(chips - 1, kind=F32)]
        + received[0],
        flops,
    )
    return grad_q, grad_k.T, grad_v.T, grad_weight


def solution(mesh):
    placed = (
        P("dp", "tensor"),
        P("dp", "tensor"),
        P("dp", "tensor"),
        P(("dp", "tensor"), None),
        P("dp", "tensor"),
    )
    return jax.shard_map(
        body,
        mesh=mesh,
        in_specs=placed,
        out_specs=(P("dp", "tensor"), P("dp", "tensor"), P("dp", "tensor"), P("dp", "tensor")),
        check_vma=False,
    )
```

```python
import functools
import math

import jax
import jax.numpy as jnp
from jax import lax
from jax.experimental import pallas as pl
from jax.experimental.pallas import tpu as pltpu
from jax.sharding import PartitionSpec as P

HEAD_DIM = 128
BLOCK = 128
VMEM_BYTES = 20 * 1024 * 1024
SLOTS = 4
SCALE = HEAD_DIM ** (-0.5)
SCALE2 = SCALE * math.log2(math.e)
VMEM = pl.BlockSpec(memory_space=pltpu.VMEM)
SMEM = pl.BlockSpec(memory_space=pltpu.SMEM)
F32 = jnp.float32
BF16 = jnp.bfloat16


def call(kernel, outs, args, flops, scratch=(), scalars=0):
    size = sum(math.prod(a.shape) * a.dtype.itemsize for a in list(args) + list(outs))
    return pl.pallas_call(
        kernel,
        out_shape=tuple(outs),
        in_specs=[SMEM] * scalars + [VMEM] * (len(args) - scalars),
        out_specs=tuple([VMEM] * len(outs)),
        scratch_shapes=list(scratch),
        cost_estimate=pl.CostEstimate(flops=flops, bytes_accessed=size // 100, transcendentals=0),
        compiler_params=pltpu.CompilerParams(vmem_limit_bytes=VMEM_BYTES),
    )(*args)


def dot(a, b, ca, cb):
    return lax.dot_general(a, b, (((ca,), (cb,)), ((), ())), preferred_element_type=F32)


def prep_kernel(order, place, keys, values, grad, own, own_kv, give):
    core, chip = place[0], place[1]
    chips, rows, width = own.shape
    half, length = keys.shape
    for k, s in enumerate(order):
        first = (chip ^ s) * 2
        own[k] = grad[:, pl.ds(pl.multiple_of((first + core) * width, 128), width)]
        own_kv[k * rows : (k + 1) * rows, :] = own[k]
        give[k] = grad[:, pl.ds(pl.multiple_of((first + 1 - core) * width, 128), width)]
    for i in range(length // width):
        at = chips * rows + i * 2 * half
        own_kv[at : at + half, :] = keys[:, i * width : (i + 1) * width]
        own_kv[at + half : at + 2 * half, :] = values[:, i * width : (i + 1) * width]


def forward_kernel(place, queries, keys, values, near, kv, attended, lse):
    parity = place[2]
    half, length = keys.shape
    depth = near.shape[1]
    mine = pl.multiple_of(parity * half, half)
    theirs = pl.multiple_of((1 - parity) * half, half)
    tail = near.shape[0] - length // depth * 2 * half
    for part, ref in enumerate((keys, values)):
        kv[part, pl.ds(mine, half), :] = ref[...]
        for i in range(length // depth):
            at = tail + (2 * i + part) * half
            kv[part, pl.ds(theirs, half), i * depth : (i + 1) * depth] = near[at : at + half, :]
    length, width = queries.shape
    row = lax.broadcasted_iota(jnp.int32, (BLOCK, BLOCK), 0)
    col = lax.broadcasted_iota(jnp.int32, (BLOCK, BLOCK), 1)
    for i in range(length // BLOCK):
        rows = pl.ds(i * BLOCK, BLOCK)
        keys = (i + 1) * BLOCK
        stats = []
        for h in range(width // HEAD_DIM):
            cols = pl.ds(h * HEAD_DIM, HEAD_DIM)
            scores = dot(queries[rows, cols], kv[0, :, :keys], 1, 0) * SCALE2
            last = jnp.where(col <= row, scores[:, keys - BLOCK :], -jnp.inf)
            top = jnp.max(last, axis=1, keepdims=True)
            if i:
                top = jnp.maximum(top, jnp.max(scores[:, : keys - BLOCK], axis=1, keepdims=True))
            powers = jnp.exp2(last - top)
            total = jnp.sum(powers, axis=1, keepdims=True)
            if i:
                early = jnp.exp2(scores[:, : keys - BLOCK] - top)
                total = total + jnp.sum(early, axis=1, keepdims=True)
                powers = jnp.concatenate([early, powers], axis=1)
            probs = (powers / total).astype(BF16)
            attended[rows, cols] = dot(probs, kv[1, :, :keys], 1, 1).astype(BF16)
            stats.append(jnp.broadcast_to(top + jnp.log2(total), (BLOCK, HEAD_DIM)))
        lane = lax.broadcasted_iota(jnp.int32, (BLOCK, HEAD_DIM), 1)
        packed = stats[0]
        for h, stat in enumerate(stats):
            packed = jnp.where(lane == h, stat, packed)
        lse[rows, :] = packed


def backward_kernel(first, final, base, place, queries, kv, lse, grad_own, grad_other, *refs):
    if not first:
        early_q, early_k, early_v = refs[:3]
        refs = refs[3:]
    if final:
        grad_q, keep, send, dk, dv = refs
    else:
        grad_q, dk, dv = refs
    if first:
        dk[...] = jnp.zeros_like(dk)
        dv[...] = jnp.zeros_like(dv)
    else:
        grad_q[...] = early_q[...]
        dk[...] = early_k[...]
        dv[...] = early_v[...]
    length, width = queries.shape
    heads = width // HEAD_DIM
    count, size, _ = grad_own.shape
    row = lax.broadcasted_iota(jnp.int32, (size, BLOCK), 0)
    col = lax.broadcasted_iota(jnp.int32, (size, BLOCK), 1)

    def block(slot, j):
        rows = pl.ds(j * size, size)
        keys = -(-(j + 1) * size // BLOCK) * BLOCK
        early = keys - BLOCK
        columns = [pl.ds(h * HEAD_DIM, HEAD_DIM) for h in range(heads)]
        lhs = [queries[rows, cols] for cols in columns]
        grads = [
            (grad_own[slot, :, cols] + grad_other[slot, :, cols].astype(F32)).astype(BF16)
            for cols in columns
        ]
        scores = [dot(value, kv[0, :, :keys], 1, 0) for value in lhs]
        dprobs = [dot(value, kv[1, :, :keys], 1, 0) for value in grads]
        halves, dscores = [], []
        for h in range(heads):
            probs = jnp.exp2(scores[h] * SCALE2 - lse[rows, h : h + 1])
            last = jnp.where(col + early <= row + j * size, probs[:, early:], 0.0)
            probs = jnp.concatenate([probs[:, :early], last], axis=1) if early else last
            delta = jnp.sum(probs * dprobs[h], axis=1, keepdims=True)
            dscores.append((probs * (dprobs[h] - delta) * SCALE).astype(BF16))
            halves.append(probs.astype(BF16))
        for h, cols in enumerate(columns):
            grad_q[rows, cols] = dot(dscores[h], kv[0, :, :keys], 1, 1).astype(BF16)
        dk[:, :keys] += dot(jnp.concatenate(lhs, axis=0), jnp.concatenate(dscores, axis=0), 0, 0)
        dv[:, :keys] += dot(jnp.concatenate(grads, axis=0), jnp.concatenate(halves, axis=0), 0, 0)

    def step(slot, carry):
        for j in range(length // size):
            pl.when(place[SLOTS + base + slot] == j)(functools.partial(block, slot, j))
        return carry

    lax.fori_loop(0, count, step, 0)
    if final:
        half = HEAD_DIM // 2
        mine = pl.ds(pl.multiple_of(place[2] * half, half), half)
        theirs = pl.ds(pl.multiple_of((1 - place[2]) * half, half), half)
        keep[:half] = dk[mine, :]
        keep[half:] = dv[mine, :]
        send[:half] = dk[theirs, :].astype(BF16)
        send[half:] = dv[theirs, :].astype(BF16)


def finish_kernel(keep, other, partial, *refs):
    received, (grad_k, grad_v, grad_weight) = refs[:-3], refs[-3:]
    half = keep.shape[0] // 2
    total = (keep[...].astype(BF16).astype(F32) + other[...].astype(F32)).astype(BF16)
    grad_k[...] = total[:half]
    grad_v[...] = total[half:]
    total = partial[...]
    for ref in received:
        total = total + ref[...].astype(F32)
    grad_weight[...] = total.astype(BF16)


def chunk(ref, c, rows):
    return ref[c] if len(ref.shape) == 3 else ref[c * rows : (c + 1) * rows, :]


def merge_kernel(first, second, *halves):
    rows = second.shape[1]
    c = 0
    for half in halves:
        for i in range(half.shape[0]):
            half[i, :rows] = chunk(first, c, rows)
            half[i, rows:] = second[c]
            c += 1


def pieces(refs, c):
    rows = refs[1].shape[1]
    return [
        jnp.concatenate([chunk(refs[i], c, rows), refs[i + 1][c]], axis=0)
        for i in range(0, len(refs), 2)
    ]


def middle_piece(place, refs, c):
    inner = (place[3] == 1) | (place[3] == 2)
    found = pieces(refs, c)
    return jnp.where(inner, found[0], found[1])


def late_piece(place, refs, i, j):
    inner = (place[3] == 1) | (place[3] == 2)
    return jnp.where(inner, refs[0][i], refs[1][j])


def attended_rows(att_own, att_other, j, rows):
    at = pl.ds(pl.multiple_of(j * rows, rows), rows)
    return jnp.concatenate([att_own[at, :], att_other[at, :]], axis=0)


def early_kernel(count, place, *refs):
    blocks, weights, (own, give) = refs[:count], refs[count:-2], refs[-2:]
    rows = own.shape[1]
    totals = None
    for c, weight in enumerate(weights):
        products = [dot(value, weight[...], 1, 0) for value in pieces(blocks, c)]
        totals = [a + b for a, b in zip(totals, products)] if totals else products
    for i, total in enumerate(totals):
        own[i] = total[:rows]
        give[i] = total[rows:].astype(BF16)


def early_term_kernel(count, place, att_own, att_other, *refs):
    blocks, outs = refs[:count], refs[count:]
    rows = blocks[1].shape[1]
    for c, out in enumerate(outs):
        total = None
        for i, value in enumerate(pieces(blocks, c)):
            product = dot(value, attended_rows(att_own, att_other, place[SLOTS + i], rows), 0, 0)
            total = product if total is None else total + product
        out[...] = total.astype(BF16)


def middle_kernel(count, place, *refs):
    middle, late, weights, out = refs[:4], refs[4:6], refs[6 : 6 + count], refs[-1]
    total = None
    for c, weight in enumerate(weights):
        product = dot(middle_piece(place, middle, c), weight[...], 1, 0)
        total = product if total is None else total + product
    out[0] = total
    total = None
    for i in range(late[0].shape[0]):
        product = dot(late_piece(place, late, i, i), weights[i][...], 1, 0)
        total = product if total is None else total + product
    out[1] = total


def late_kernel(chunks, place, *refs):
    count = len(chunks)
    late, weights = refs[: 2 * count], refs[2 * count : 3 * count]
    early, own, give = refs[3 * count :]
    total = early[1]
    for c, (i, j) in enumerate(chunks):
        total += dot(late_piece(place, late[2 * c : 2 * c + 2], i, j), weights[c][...], 1, 0)
    rows = own.shape[1]
    for q, value in enumerate((early[0], total)):
        own[q] = value[:rows]
        give[q] = value[rows:].astype(BF16)


def term_kernel(c, i, j, late, count, place, att_own, att_other, partial, *refs):
    blocks, received, outs = refs[:late], refs[late : late + count], refs[late + count :]
    total = partial[...].astype(F32)
    if late:
        values = [middle_piece(place, blocks[:4], c), late_piece(place, blocks[4:], i, j)]
        rows = values[0].shape[0] // 2
        slots = [place[place.shape[0] - 2], place[place.shape[0] - 1]]
        for slot, value in zip(slots, values):
            total = total + dot(value, attended_rows(att_own, att_other, slot, rows), 0, 0)
    for ref in received:
        total = total + ref[...].astype(F32)
    outs[0][...] = total.astype(outs[0].dtype)


def tie(value, *others):
    return lax.optimization_barrier((value, *others))[0]


def body(queries, keys, values, grad_out, out_weight):
    dp, tensor = lax.axis_size("dp"), lax.axis_size("tensor")
    chips = dp // 2
    length, width = queries.shape
    half = keys.shape[1]
    rows = grad_out.shape[0]
    depth = out_weight.shape[0]
    index, part = lax.axis_index("dp"), lax.axis_index("tensor")
    if tensor == 4:
        inner = (part == 1) | (part == 2)
        early = 2
        slots = [0, 1, jnp.where(inner, 3, 2), jnp.where(inner, 2, 3)]
    else:
        early = tensor
        slots = list(range(tensor))
    place = jnp.stack(
        [index % 2, index // 2, part % 2, part] + [part ^ k for k in slots]
    ).astype(jnp.int32)

    def swap(value, axis, mask):
        return lax.ppermute(value, axis, [(i, i ^ mask) for i in range(lax.axis_size(axis))])

    def across(value):
        return lax.ppermute(value, "tensor", [(1, 2), (2, 1)])

    def outward(value):
        return lax.ppermute(value, "tensor", [(1, 0), (2, 3)])

    shape = jax.ShapeDtypeStruct
    order = sorted(range(chips), key=lambda s: (-s.bit_count(), s))
    half_block = shape((chips, rows, depth), BF16)
    tail = length // depth * 2 * half
    own, own_kv, give = call(
        functools.partial(prep_kernel, order),
        [half_block, shape((chips * rows + tail, depth), BF16), half_block],
        [place, keys.T, values.T, grad_out],
        0,
        scalars=1,
    )
    taken = swap(give, "dp", 1)

    near = [swap(own_kv, "tensor", 1), swap(taken, "tensor", 1)]
    weights = {0: out_weight}
    for s in reversed(order[:-1]):
        operand = out_weight if s & (s - 1) else tie(out_weight, near[0])
        weights[s] = swap(operand, "dp", 2 * s)
    weights = [weights[s] for s in order]

    blocks = [own_kv, taken] + near
    late, second = [], []
    sizes = [1, chips - 2, 1] if chips > 2 else [1] * chips
    flops = 4 * length * depth * width // 100
    if tensor == 4:
        middle_own = across(own)
        direct = [w for s, w in zip(order, weights) if s & (s - 1)]
        middle_taken = across(taken)
        hold = []
        kv, attended, lse = call(
            forward_kernel,
            [
                shape((2, HEAD_DIM, length), BF16),
                shape((length, width), BF16),
                shape((length, HEAD_DIM), F32),
            ],
            [place, tie(queries, *hold), keys.T, values.T, near[0]],
            4 * length * length * width // 100,
            scalars=1,
        )
        in_own = outward(middle_own)
        in_taken = outward(tie(middle_taken, near[1]))
        middle = [middle_own, middle_taken, in_own, in_taken]
        att_other = swap(attended, "dp", 1)
        relay = call(
            merge_kernel,
            [shape((size, 2 * rows, depth), BF16) for size in sizes],
            near,
            400 * flops,
        )
        after = [[middle_taken, att_other, *direct], [in_own, *weights], []]
        for side in range(len(sizes)):
            second.append(across(tie(relay[side], *after[side], *second[-1:])))
    else:
        hold = []
        kv, attended, lse = call(
            forward_kernel,
            [
                shape((2, HEAD_DIM, length), BF16),
                shape((length, width), BF16),
                shape((length, HEAD_DIM), F32),
            ],
            [place, tie(queries, *hold), keys.T, values.T, near[0]],
            4 * length * length * width // 100,
            scalars=1,
        )
        att_other = swap(attended, "dp", 1)
        for k in range(2, tensor):
            blocks += [swap(own, "tensor", k), swap(taken, "tensor", k)]
    grad_own, grad_give = call(
        functools.partial(early_kernel, len(blocks)),
        [shape((early, rows, width), F32), shape((early, rows, width), BF16)],
        [place] + blocks + weights,
        300 * flops,
        scalars=1,
    )
    partials = call(
        functools.partial(early_term_kernel, len(blocks)),
        [shape((depth, width), BF16)] * chips,
        [tie(place, grad_give), attended, att_other] + blocks,
        flops,
        scalars=1,
    )
    grad_other = swap(grad_give, "dp", 1)
    def backward(first, final, base, own, other, carry):
        state = [shape((HEAD_DIM, length), F32)] * 2
        ends = [shape((2 * half, length), F32), shape((2 * half, length), BF16)]
        scratch = [pltpu.VMEM((HEAD_DIM, length), F32)] * 2 if final else []
        return call(
            functools.partial(backward_kernel, first, final, base),
            [shape((length, width), BF16)] + (ends if final else state),
            [place, queries, kv, lse, own, other] + carry,
            flops,
            scratch=scratch,
            scalars=1,
        )

    done = backward(True, early == tensor, 0, grad_own, grad_other, [])
    if tensor == 4:
        after = [[], [in_taken, partials[0], done[1]], []]
        for side, size in enumerate(sizes):
            arrived = outward(tie(second[side], *after[side]))
            late += [(i, i, [second[side], arrived]) for i in range(size)]
    else:
        late = [(0, 0, [])] * chips
        middle = []


    received = {s: [] for s in order}

    def term(c, *others, kind=BF16):
        s = order[c]
        extra = received[s] if s else []
        (found,) = call(
            functools.partial(
                term_kernel, c, *late[c][:2], len(middle + late[c][2]), len(extra)
            ),
            [shape((depth, width), kind)],
            [tie(place, *others), attended, att_other, partials[c]]
            + middle
            + late[c][2]
            + extra,
            300 * flops,
            scalars=1,
        )
        if s:
            low = s & -s
            received[s ^ low].append(swap(found, "dp", 2 * low))
        return found

    terms = [term(0)]
    total = place
    if tensor == 4:
        (total,) = call(
            functools.partial(middle_kernel, chips),
            [shape((2, 2 * rows, width), F32)],
            [tie(place, terms[0])] + middle + late[0][2] + weights,
            flops,
            scalars=1,
        )
    terms += [term(c, total) for c in range(1, chips - 1)]

    if tensor == 4:
        ends = late[sizes[0] :]
        grad_own, grad_give = call(
            functools.partial(late_kernel, [item[:2] for item in ends]),
            [shape((2, rows, width), F32), shape((2, rows, width), BF16)],
            [place] + sum([item[2] for item in ends], []) + weights[sizes[0] :] + [total],
            flops,
            scalars=1,
        )
        grad_other = swap(grad_give, "dp", 1)
        done = backward(False, True, early, grad_own, grad_other, list(done))
    grad_q, keep, send = done
    grad_k, grad_v, grad_weight = call(
        finish_kernel,
        [shape((half, length), BF16)] * 2 + [shape((depth, width), BF16)],
        [keep, swap(send, "tensor", 1), term(chips - 1, kind=F32)]
        + received[0],
        flops,
    )
    return grad_q, grad_k.T, grad_v.T, grad_weight


def solution(mesh):
    placed = (
        P("dp", "tensor"),
        P("dp", "tensor"),
        P("dp", "tensor"),
        P(("dp", "tensor"), None),
        P("dp", "tensor"),
    )
    return jax.shard_map(
        body,
        mesh=mesh,
        in_specs=placed,
        out_specs=(P("dp", "tensor"), P("dp", "tensor"), P("dp", "tensor"), P("dp", "tensor")),
        check_vma=False,
    )
```

```python
import functools
import math

import jax
import jax.numpy as jnp
from jax import lax
from jax.experimental import pallas as pl
from jax.experimental.pallas import tpu as pltpu
from jax.sharding import PartitionSpec as P

HEAD_DIM = 128
BLOCK = 128
VMEM_BYTES = 20 * 1024 * 1024
SLOTS = 4
SCALE = HEAD_DIM ** (-0.5)
SCALE2 = SCALE * math.log2(math.e)
VMEM = pl.BlockSpec(memory_space=pltpu.VMEM)
SMEM = pl.BlockSpec(memory_space=pltpu.SMEM)
F32 = jnp.float32
BF16 = jnp.bfloat16


def call(kernel, outs, args, flops, scratch=(), scalars=0):
    size = sum(math.prod(a.shape) * a.dtype.itemsize for a in list(args) + list(outs))
    return pl.pallas_call(
        kernel,
        out_shape=tuple(outs),
        in_specs=[SMEM] * scalars + [VMEM] * (len(args) - scalars),
        out_specs=tuple([VMEM] * len(outs)),
        scratch_shapes=list(scratch),
        cost_estimate=pl.CostEstimate(flops=flops, bytes_accessed=size // 100, transcendentals=0),
        compiler_params=pltpu.CompilerParams(vmem_limit_bytes=VMEM_BYTES),
    )(*args)


def dot(a, b, ca, cb):
    return lax.dot_general(a, b, (((ca,), (cb,)), ((), ())), preferred_element_type=F32)


def prep_kernel(order, place, keys, values, grad, own, own_kv, give):
    core, chip = place[0], place[1]
    chips, rows, width = own.shape
    half, length = keys.shape
    for k, s in enumerate(order):
        first = (chip ^ s) * 2
        own[k] = grad[:, pl.ds(pl.multiple_of((first + core) * width, 128), width)]
        own_kv[k * rows : (k + 1) * rows, :] = own[k]
        give[k] = grad[:, pl.ds(pl.multiple_of((first + 1 - core) * width, 128), width)]
    for i in range(length // width):
        at = chips * rows + i * 2 * half
        own_kv[at : at + half, :] = keys[:, i * width : (i + 1) * width]
        own_kv[at + half : at + 2 * half, :] = values[:, i * width : (i + 1) * width]


def forward_kernel(place, queries, keys, values, near, kv, attended, lse):
    parity = place[2]
    half, length = keys.shape
    depth = near.shape[1]
    mine = pl.multiple_of(parity * half, half)
    theirs = pl.multiple_of((1 - parity) * half, half)
    tail = near.shape[0] - length // depth * 2 * half
    for part, ref in enumerate((keys, values)):
        kv[part, pl.ds(mine, half), :] = ref[...]
        for i in range(length // depth):
            at = tail + (2 * i + part) * half
            kv[part, pl.ds(theirs, half), i * depth : (i + 1) * depth] = near[at : at + half, :]
    length, width = queries.shape
    row = lax.broadcasted_iota(jnp.int32, (BLOCK, BLOCK), 0)
    col = lax.broadcasted_iota(jnp.int32, (BLOCK, BLOCK), 1)
    for i in range(length // BLOCK):
        rows = pl.ds(i * BLOCK, BLOCK)
        keys = (i + 1) * BLOCK
        stats = []
        for h in range(width // HEAD_DIM):
            cols = pl.ds(h * HEAD_DIM, HEAD_DIM)
            scores = dot(queries[rows, cols], kv[0, :, :keys], 1, 0) * SCALE2
            last = jnp.where(col <= row, scores[:, keys - BLOCK :], -jnp.inf)
            top = jnp.max(last, axis=1, keepdims=True)
            if i:
                top = jnp.maximum(top, jnp.max(scores[:, : keys - BLOCK], axis=1, keepdims=True))
            powers = jnp.exp2(last - top)
            total = jnp.sum(powers, axis=1, keepdims=True)
            if i:
                early = jnp.exp2(scores[:, : keys - BLOCK] - top)
                total = total + jnp.sum(early, axis=1, keepdims=True)
                powers = jnp.concatenate([early, powers], axis=1)
            probs = (powers / total).astype(BF16)
            attended[rows, cols] = dot(probs, kv[1, :, :keys], 1, 1).astype(BF16)
            stats.append(jnp.broadcast_to(top + jnp.log2(total), (BLOCK, HEAD_DIM)))
        lane = lax.broadcasted_iota(jnp.int32, (BLOCK, HEAD_DIM), 1)
        packed = stats[0]
        for h, stat in enumerate(stats):
            packed = jnp.where(lane == h, stat, packed)
        lse[rows, :] = packed


def backward_kernel(first, final, base, place, queries, kv, lse, grad_own, grad_other, *refs):
    if not first:
        early_q, early_k, early_v = refs[:3]
        refs = refs[3:]
    if final:
        grad_q, keep, send, dk, dv = refs
    else:
        grad_q, dk, dv = refs
    if first:
        dk[...] = jnp.zeros_like(dk)
        dv[...] = jnp.zeros_like(dv)
    else:
        grad_q[...] = early_q[...]
        dk[...] = early_k[...]
        dv[...] = early_v[...]
    length, width = queries.shape
    heads = width // HEAD_DIM
    count, size, _ = grad_own.shape
    row = lax.broadcasted_iota(jnp.int32, (size, BLOCK), 0)
    col = lax.broadcasted_iota(jnp.int32, (size, BLOCK), 1)

    def block(slot, j):
        rows = pl.ds(j * size, size)
        keys = -(-(j + 1) * size // BLOCK) * BLOCK
        early = keys - BLOCK
        columns = [pl.ds(h * HEAD_DIM, HEAD_DIM) for h in range(heads)]
        lhs = [queries[rows, cols] for cols in columns]
        grads = [
            (grad_own[slot, :, cols] + grad_other[slot, :, cols].astype(F32)).astype(BF16)
            for cols in columns
        ]
        scores = [dot(value, kv[0, :, :keys], 1, 0) for value in lhs]
        dprobs = [dot(value, kv[1, :, :keys], 1, 0) for value in grads]
        halves, dscores = [], []
        for h in range(heads):
            probs = jnp.exp2(scores[h] * SCALE2 - lse[rows, h : h + 1])
            last = jnp.where(col + early <= row + j * size, probs[:, early:], 0.0)
            probs = jnp.concatenate([probs[:, :early], last], axis=1) if early else last
            delta = jnp.sum(probs * dprobs[h], axis=1, keepdims=True)
            dscores.append((probs * (dprobs[h] - delta) * SCALE).astype(BF16))
            halves.append(probs.astype(BF16))
        for h, cols in enumerate(columns):
            grad_q[rows, cols] = dot(dscores[h], kv[0, :, :keys], 1, 1).astype(BF16)
        dk[:, :keys] += dot(jnp.concatenate(lhs, axis=0), jnp.concatenate(dscores, axis=0), 0, 0)
        dv[:, :keys] += dot(jnp.concatenate(grads, axis=0), jnp.concatenate(halves, axis=0), 0, 0)

    def step(slot, carry):
        for j in range(length // size):
            pl.when(place[SLOTS + base + slot] == j)(functools.partial(block, slot, j))
        return carry

    lax.fori_loop(0, count, step, 0)
    if final:
        half = HEAD_DIM // 2
        mine = pl.ds(pl.multiple_of(place[2] * half, half), half)
        theirs = pl.ds(pl.multiple_of((1 - place[2]) * half, half), half)
        keep[:half] = dk[mine, :]
        keep[half:] = dv[mine, :]
        send[:half] = dk[theirs, :].astype(BF16)
        send[half:] = dv[theirs, :].astype(BF16)


def finish_kernel(keep, other, partial, *refs):
    received, (grad_k, grad_v, grad_weight) = refs[:-3], refs[-3:]
    half = keep.shape[0] // 2
    total = (keep[...].astype(BF16).astype(F32) + other[...].astype(F32)).astype(BF16)
    grad_k[...] = total[:half]
    grad_v[...] = total[half:]
    total = partial[...]
    for ref in received:
        total = total + ref[...].astype(F32)
    grad_weight[...] = total.astype(BF16)


def chunk(ref, c, rows):
    return ref[c] if len(ref.shape) == 3 else ref[c * rows : (c + 1) * rows, :]


def merge_kernel(first, second, *halves):
    rows = second.shape[1]
    c = 0
    for half in halves:
        for i in range(half.shape[0]):
            half[i, :rows] = chunk(first, c, rows)
            half[i, rows:] = second[c]
            c += 1


def pieces(refs, c):
    rows = refs[1].shape[1]
    return [
        jnp.concatenate([chunk(refs[i], c, rows), refs[i + 1][c]], axis=0)
        for i in range(0, len(refs), 2)
    ]


def middle_piece(place, refs, c):
    inner = (place[3] == 1) | (place[3] == 2)
    found = pieces(refs, c)
    return jnp.where(inner, found[0], found[1])


def late_piece(place, refs, i, j):
    inner = (place[3] == 1) | (place[3] == 2)
    return jnp.where(inner, refs[0][i], refs[1][j])


def attended_rows(att_own, att_other, j, rows):
    at = pl.ds(pl.multiple_of(j * rows, rows), rows)
    return jnp.concatenate([att_own[at, :], att_other[at, :]], axis=0)


def early_kernel(count, place, *refs):
    blocks, weights, (own, give) = refs[:count], refs[count:-2], refs[-2:]
    rows = own.shape[1]
    totals = None
    for c, weight in enumerate(weights):
        products = [dot(value, weight[...], 1, 0) for value in pieces(blocks, c)]
        totals = [a + b for a, b in zip(totals, products)] if totals else products
    for i, total in enumerate(totals):
        own[i] = total[:rows]
        give[i] = total[rows:].astype(BF16)


def early_term_kernel(count, place, att_own, att_other, *refs):
    blocks, outs = refs[:count], refs[count:]
    rows = blocks[1].shape[1]
    for c, out in enumerate(outs):
        total = None
        for i, value in enumerate(pieces(blocks, c)):
            product = dot(value, attended_rows(att_own, att_other, place[SLOTS + i], rows), 0, 0)
            total = product if total is None else total + product
        out[...] = total.astype(BF16)


def middle_kernel(count, place, *refs):
    middle, late, weights, out = refs[:4], refs[4:6], refs[6 : 6 + count], refs[-1]
    total = None
    for c, weight in enumerate(weights):
        product = dot(middle_piece(place, middle, c), weight[...], 1, 0)
        total = product if total is None else total + product
    out[0] = total
    total = None
    for i in range(late[0].shape[0]):
        product = dot(late_piece(place, late, i, i), weights[i][...], 1, 0)
        total = product if total is None else total + product
    out[1] = total


def late_kernel(chunks, place, *refs):
    count = len(chunks)
    late, weights = refs[: 2 * count], refs[2 * count : 3 * count]
    early, own, give = refs[3 * count :]
    total = early[1]
    for c, (i, j) in enumerate(chunks):
        total += dot(late_piece(place, late[2 * c : 2 * c + 2], i, j), weights[c][...], 1, 0)
    rows = own.shape[1]
    for q, value in enumerate((early[0], total)):
        own[q] = value[:rows]
        give[q] = value[rows:].astype(BF16)


def term_kernel(c, i, j, late, spans, place, att_own, att_other, partial, *refs):
    blocks, received = refs[:late], refs[late : late + len(spans)]
    outs = refs[late + len(spans) :]
    total = partial[...].astype(F32)
    if late:
        values = [middle_piece(place, blocks[:4], c), late_piece(place, blocks[4:], i, j)]
        rows = values[0].shape[0] // 2
        slots = [place[place.shape[0] - 2], place[place.shape[0] - 1]]
        for slot, value in zip(slots, values):
            total = total + dot(value, attended_rows(att_own, att_other, slot, rows), 0, 0)
    middle = total.shape[0] // 2
    sides = [total[:middle], total[middle:]]
    for ref, span in zip(received, spans):
        for side in span:
            part = ref[...] if len(span) == 1 else ref[side * middle : (side + 1) * middle]
            sides[side] = sides[side] + part.astype(F32)
    if len(outs) == 2:
        for out, side in zip(outs, sides):
            out[...] = side.astype(out.dtype)
    else:
        outs[0][:middle] = sides[0].astype(outs[0].dtype)
        outs[0][middle:] = sides[1].astype(outs[0].dtype)


def tie(value, *others):
    return lax.optimization_barrier((value, *others))[0]


def body(queries, keys, values, grad_out, out_weight):
    dp, tensor = lax.axis_size("dp"), lax.axis_size("tensor")
    chips = dp // 2
    length, width = queries.shape
    half = keys.shape[1]
    rows = grad_out.shape[0]
    depth = out_weight.shape[0]
    index, part = lax.axis_index("dp"), lax.axis_index("tensor")
    if tensor == 4:
        inner = (part == 1) | (part == 2)
        early = 2
        slots = [0, 1, jnp.where(inner, 3, 2), jnp.where(inner, 2, 3)]
    else:
        early = tensor
        slots = list(range(tensor))
    place = jnp.stack(
        [index % 2, index // 2, part % 2, part] + [part ^ k for k in slots]
    ).astype(jnp.int32)

    def swap(value, axis, mask):
        return lax.ppermute(value, axis, [(i, i ^ mask) for i in range(lax.axis_size(axis))])

    def across(value):
        return lax.ppermute(value, "tensor", [(1, 2), (2, 1)])

    def outward(value):
        return lax.ppermute(value, "tensor", [(1, 0), (2, 3)])

    shape = jax.ShapeDtypeStruct
    order = sorted(range(chips), key=lambda s: (-s.bit_count(), s))
    half_block = shape((chips, rows, depth), BF16)
    tail = length // depth * 2 * half
    own, own_kv, give = call(
        functools.partial(prep_kernel, order),
        [half_block, shape((chips * rows + tail, depth), BF16), half_block],
        [place, keys.T, values.T, grad_out],
        0,
        scalars=1,
    )
    taken = swap(give, "dp", 1)

    near = [swap(own_kv, "tensor", 1), swap(taken, "tensor", 1)]
    weights = {0: out_weight}
    for s in reversed(order[:-1]):
        operand = out_weight if s & (s - 1) else tie(out_weight, near[0])
        weights[s] = swap(operand, "dp", 2 * s)
    weights = [weights[s] for s in order]

    blocks = [own_kv, taken] + near
    late, second = [], []
    sizes = [1, chips - 2, 1] if chips > 2 else [1] * chips
    flops = 4 * length * depth * width // 100
    if tensor == 4:
        middle_own = across(own)
        direct = [w for s, w in zip(order, weights) if s & (s - 1)]
        middle_taken = across(taken)
        hold = []
        kv, attended, lse = call(
            forward_kernel,
            [
                shape((2, HEAD_DIM, length), BF16),
                shape((length, width), BF16),
                shape((length, HEAD_DIM), F32),
            ],
            [place, tie(queries, *hold), keys.T, values.T, near[0]],
            4 * length * length * width // 100,
            scalars=1,
        )
        in_own = outward(middle_own)
        in_taken = outward(tie(middle_taken, near[1]))
        middle = [middle_own, middle_taken, in_own, in_taken]
        att_other = swap(attended, "dp", 1)
        relay = call(
            merge_kernel,
            [shape((size, 2 * rows, depth), BF16) for size in sizes],
            near,
            400 * flops,
        )
        after = [[middle_taken, att_other, *direct], [in_own, weights[0]], []]
        for side in range(len(sizes)):
            second.append(across(tie(relay[side], *after[side], *second[-1:])))
    else:
        hold = []
        kv, attended, lse = call(
            forward_kernel,
            [
                shape((2, HEAD_DIM, length), BF16),
                shape((length, width), BF16),
                shape((length, HEAD_DIM), F32),
            ],
            [place, tie(queries, *hold), keys.T, values.T, near[0]],
            4 * length * length * width // 100,
            scalars=1,
        )
        att_other = swap(attended, "dp", 1)
        for k in range(2, tensor):
            blocks += [swap(own, "tensor", k), swap(taken, "tensor", k)]
    grad_own, grad_give = call(
        functools.partial(early_kernel, len(blocks)),
        [shape((early, rows, width), F32), shape((early, rows, width), BF16)],
        [place] + blocks + weights,
        300 * flops,
        scalars=1,
    )
    partials = call(
        functools.partial(early_term_kernel, len(blocks)),
        [shape((depth, width), BF16)] * chips,
        [tie(place, grad_give), attended, att_other] + blocks,
        flops,
        scalars=1,
    )
    grad_other = swap(grad_give, "dp", 1)
    def backward(first, final, base, own, other, carry):
        state = [shape((HEAD_DIM, length), F32)] * 2
        ends = [shape((2 * half, length), F32), shape((2 * half, length), BF16)]
        scratch = [pltpu.VMEM((HEAD_DIM, length), F32)] * 2 if final else []
        return call(
            functools.partial(backward_kernel, first, final, base),
            [shape((length, width), BF16)] + (ends if final else state),
            [place, queries, kv, lse, own, other] + carry,
            flops,
            scratch=scratch,
            scalars=1,
        )

    done = backward(True, early == tensor, 0, grad_own, grad_other, [])
    if tensor == 4:
        after = [[], [in_taken, partials[0], done[1]], []]
        for side, size in enumerate(sizes):
            arrived = outward(tie(second[side], *after[side]))
            late += [(i, i, [second[side], arrived]) for i in range(size)]
    else:
        late = [(0, 0, [])] * chips
        middle = []


    received = {s: [] for s in order}

    def term(c, *others, kind=BF16):
        s = order[c]
        low, high = s & -s, 1 << s.bit_length() >> 1
        spans, extra = zip(*received[s]) if received[s] and s else ((), ())
        shapes = [(depth, width)] if low == high else [(depth // 2, width)] * 2
        found = call(
            functools.partial(term_kernel, c, *late[c][:2], len(middle + late[c][2]), spans),
            [shape(size, kind) for size in shapes],
            [tie(place, *others), attended, att_other, partials[c]]
            + middle
            + late[c][2]
            + list(extra),
            300 * flops,
            scalars=1,
        )
        if len(found) == 2:
            received[s ^ low].append(((0,), swap(found[0], "dp", 2 * low)))
            received[s ^ high].append(((1,), swap(found[1], "dp", 2 * high)))
        elif s:
            received[0].append(((0, 1), swap(found[0], "dp", 2 * s)))
        return found[0]

    terms = [term(0)]
    total = place
    if tensor == 4:
        (total,) = call(
            functools.partial(middle_kernel, chips),
            [shape((2, 2 * rows, width), F32)],
            [tie(place, terms[0])] + middle + late[0][2] + weights,
            flops,
            scalars=1,
        )
    terms += [term(c, total) for c in range(1, chips - 1)]

    if tensor == 4:
        ends = late[sizes[0] :]
        grad_own, grad_give = call(
            functools.partial(late_kernel, [item[:2] for item in ends]),
            [shape((2, rows, width), F32), shape((2, rows, width), BF16)],
            [place] + sum([item[2] for item in ends], []) + weights[sizes[0] :] + [total],
            flops,
            scalars=1,
        )
        grad_other = swap(grad_give, "dp", 1)
        done = backward(False, True, early, grad_own, grad_other, list(done))
    grad_q, keep, send = done
    grad_k, grad_v, grad_weight = call(
        finish_kernel,
        [shape((half, length), BF16)] * 2 + [shape((depth, width), BF16)],
        [keep, swap(send, "tensor", 1), term(chips - 1, kind=F32)]
        + [value for _, value in received[0]],
        flops,
    )
    return grad_q, grad_k.T, grad_v.T, grad_weight


def solution(mesh):
    placed = (
        P("dp", "tensor"),
        P("dp", "tensor"),
        P("dp", "tensor"),
        P(("dp", "tensor"), None),
        P("dp", "tensor"),
    )
    return jax.shard_map(
        body,
        mesh=mesh,
        in_specs=placed,
        out_specs=(P("dp", "tensor"), P("dp", "tensor"), P("dp", "tensor"), P("dp", "tensor")),
        check_vma=False,
    )
```
